32 devices in a mesh: grp: 2 (over x), chan: 16 (over z, y, core).
Axes of the slice: x: 2, y: 2, z: 4, core: 2. Of those that a mesh axis runs over, the one named last changes fastest.
Arguments:
- voltages: bfloat16 [8, 16384, 2048], P('grp', 'chan'), parts along dimension 0, may hold values from -6 to 6
- delay_step: int32 [16384], replicated, may hold values from 0 to 1048575
- trials: int32 [256], replicated, may hold values from 0 to 2047
Outputs:
- spectra: float32 [48, 2, 8, 256], P('chan', None, 'grp'), parts along dimension 2
- power: float32 [8, 256], P('grp', 'chan'), parts along dimension 0
The draws below stay inside these ranges and needn't reach their ends.
There are 2 independent parts, one for each index of `grp`. The reference program is written for one: setup_inputs(seed, part) draws one part's arguments, and reference() takes and returns one part's arrays. A program takes and returns all parts, laid end to end along the dimension named above; an argument that names none is the same for every part. Nothing has to cross between parts.
All inputs are finite; a program needn't handle non-finite values.
Results may differ from the reference program's by a relative error of at most 0.0037.
Values may be sent and summed in bfloat16 or wider, within the bound.
A program may use at most 64 MiB of HBM per device.

```python
import math
import jax
import jax.numpy as jnp
from jax import lax

B = 4
CHANNELS = 16384
SAMPLES = 2048
SUBSTEPS = 512
TRIALS = 256
BINS = 48


def draw_delay_step(key, part):
    base_key = jax.random.fold_in(key, 4711)
    band_key, offset_key, pick_key = jax.random.split(base_key, 3)
    band_low = jax.random.randint(band_key, (), 2 * CHANNELS, 4 * CHANNELS, dtype=jnp.int32)
    channel_index = jnp.arange(CHANNELS, dtype=jnp.int32)
    frequency = band_low + channel_index
    band_top = band_low + CHANNELS
    gap_index = band_top - frequency
    scaled_gap = 4 * SAMPLES * gap_index // frequency
    coarse_delay = scaled_gap * (band_top + frequency) // (4 * frequency)
    sub_sample = jax.random.randint(offset_key, (CHANNELS,), 0, SUBSTEPS, dtype=jnp.int32)
    values = coarse_delay % SAMPLES * SUBSTEPS + sub_sample
    chosen = jax.random.randint(pick_key, (), 0, CHANNELS - 1, dtype=jnp.int32)
    values = jnp.where(channel_index == chosen, SAMPLES * SUBSTEPS - 1, values)
    values = jnp.where(channel_index == CHANNELS - 1, 0, values)
    return values.astype(jnp.int32)


def touch_ends(drawn, own_key, low, top_value):
    shape = drawn.shape
    place = [jax.random.randint(jax.random.fold_in(own_key, axis), (), 0, shape[axis]) for axis in range(len(shape))]
    drawn = drawn.at[tuple(place)].set(low)
    longest = shape.index(max(shape))
    place[longest] = (place[longest] + 1) % shape[longest]
    return drawn.at[tuple(place)].set(top_value)


def steps_of(own_key, shape, shards, smallest, top_value):
    loudness, own = 1.0, jax.random.fold_in(own_key, 6)
    for dim, shards_of in shards:
        heights = jnp.exp(jax.random.uniform(jax.random.fold_in(own, dim), (shards_of,), jnp.float32, smallest / len(shards), top_value / len(shards)))
        loudness = loudness * jnp.repeat(heights, shape[dim] // shards_of).reshape([-1 if axis == dim else 1 for axis in range(len(shape))])
    return loudness


def normal_values(stream_key, extent, spread, most, pieces=(), kind=jnp.bfloat16):
    result = spread * jax.random.normal(stream_key, extent, jnp.float32)
    if pieces:
        result = result * steps_of(stream_key, extent, pieces, -0.22, 0.18)
    return jnp.clip(result, -most, most).astype(kind)


def setup_inputs(seed: int = 0, part: int = 0) -> dict:
    key_list = jax.random.split(jax.random.key(seed), 4)
    part_splits = jax.random.split(jax.random.fold_in(key_list[3], part), 4)
    voltages = normal_values(part_splits[0], (B, CHANNELS, SAMPLES), 1.0, 6.0, ((1, 16),))
    delay_step = draw_delay_step(jax.random.fold_in(key_list[3], 71), part)
    trials = touch_ends(jax.random.randint(key_list[2], (TRIALS,), 0, SAMPLES), jax.random.fold_in(key_list[2], 1), 0, SAMPLES - 1).astype(jnp.int32)
    return dict(voltages=voltages, delay_step=delay_step, trials=trials)


def build_table(samples, bins):
    times = jnp.arange(samples, dtype=jnp.int32)
    frequency = jnp.arange(bins, dtype=jnp.int32)
    phase_index = times[:, None] * frequency[None, :] % samples
    angles = phase_index.astype(jnp.float32) * (2.0 * math.pi / samples)
    return jnp.concatenate([jnp.cos(angles), -jnp.sin(angles)], axis=1).astype(jnp.bfloat16)

def make_phases(spin_bin, delay_step, trials, modulus):
    chan_phase = spin_bin * delay_step % modulus
    phase_index = chan_phase[:, None] * trials[None, :] % modulus
    angles = phase_index.astype(jnp.float32) * (2.0 * math.pi / modulus)
    return jnp.concatenate([jnp.cos(angles), jnp.sin(angles)], axis=1)

def reference(voltages, delay_step, trials):
    modulus = SAMPLES * SUBSTEPS
    dft_table = build_table(SAMPLES, BINS).astype(jnp.float32)
    spectrum = jnp.einsum('tg,bct->gbc', dft_table, voltages.astype(jnp.float32))
    spectrum = (spectrum * (1.0 / math.sqrt(SAMPLES))).astype(jnp.bfloat16)
    spectrum = spectrum.reshape(2, BINS, B, CHANNELS)
    chan_scale = 1.0 / math.sqrt(CHANNELS)

    def one_bin(spin_bin):
        pair_rows = lax.dynamic_index_in_dim(spectrum, spin_bin, axis=1, keepdims=False).reshape(2 * B, CHANNELS)
        pair_rows = pair_rows.astype(jnp.float32)
        phases = make_phases(spin_bin, delay_step, trials, modulus)
        product = jnp.dot(pair_rows, phases, precision=lax.Precision.HIGHEST, preferred_element_type=jnp.float32)
        real_rows = product[:B]
        imag_rows = product[B:]
        real_out = real_rows[:, :TRIALS] - imag_rows[:, TRIALS:]
        imag_out = real_rows[:, TRIALS:] + imag_rows[:, :TRIALS]
        return jnp.stack([real_out, imag_out]) * chan_scale
    spectra = lax.map(one_bin, jnp.arange(BINS, dtype=jnp.int32))
    power = lax.optimization_barrier(jnp.sum(spectra * spectra, axis=(0, 1))) / BINS
    return (spectra, power)
```

```python
import functools
import math

import jax
import jax.numpy as jnp
import numpy as np
from jax import lax
from jax.experimental import pallas as pl
from jax.experimental.pallas import tpu as pltpu
from jax.sharding import PartitionSpec as P

SUBSTEPS = 512
SPIN_DEV = 3
CHUNK = 256
FINE = 64
COARSE = 8
UNROLL = 6


def padded(count):
    return -(-count // 128) * 128


def build_table(samples, bins):
    index = np.arange(samples)[:, None] * np.arange(bins)[None, :] % samples
    angles = index * (2.0 * math.pi / samples)
    table = np.zeros((samples, padded(2 * bins)), np.float32)
    table[:, :bins] = np.cos(angles)
    table[:, bins : 2 * bins] = -np.sin(angles)
    return jnp.asarray(table.astype(jnp.bfloat16))


def unit_phase(product, shift):
    turns = lax.shift_left(product, jnp.int32(shift)).astype(jnp.float32)
    half = turns * (math.pi * 2.0**-32)
    square = half * half
    sine, cosine = jnp.float32(0), jnp.float32(0)
    for power in (11, 9, 7, 5, 3, 1):
        sine = sine * square + (-1.0) ** (power // 2) / math.factorial(power)
    for power in (12, 10, 8, 6, 4, 2, 0):
        cosine = cosine * square + (-1.0) ** (power // 2) / math.factorial(power)
    sine = sine * half
    return 1.0 - 2.0 * sine * sine, 2.0 * sine * cosine


def local_kernel(
    bins, chan_total, v_ref, table_ref, delay_ref, trials_ref, out_ref, acc, spec, turn
):
    beams, chunk, samples = v_ref.shape
    steps = pl.num_programs(0)
    step = pl.program_id(0)
    shift = 32 - (samples * SUBSTEPS * 2).bit_length() + 1
    delay = delay_ref[...]

    @pl.when(step == 0)
    def _():
        acc[...] = jnp.zeros_like(acc)

    bin_delay = lax.broadcasted_iota(jnp.int32, (bins, chunk), 0) * delay
    mid_cos, mid_sin = unit_phase(bin_delay * (samples - 1), shift)
    for jump in range(4):
        jump_cos, jump_sin = unit_phase(bin_delay * (32 * (jump + 1)), shift)
        turn[2 * jump] = jump_cos
        turn[2 * jump + 1] = jump_sin
    for beam in range(beams):
        rows = jnp.dot(v_ref[beam], table_ref[...], preferred_element_type=jnp.float32)
        rows = (rows.T * (1.0 / math.sqrt(samples))).astype(jnp.bfloat16).astype(jnp.float32)
        real, imag = rows[:bins], rows[bins : 2 * bins]
        spec[beam] = real * mid_cos - imag * mid_sin
        spec[beams + beam] = real * mid_sin + imag * mid_cos

    odd = 2 * lax.broadcasted_iota(jnp.int32, (8, chunk), 0) + 1
    fine_rc, fine_rs = unit_phase(odd * delay, shift)
    coarse_rc, coarse_rs = unit_phase(odd * (2 * FINE) * delay, shift)

    def one_bin(spin_bin, carry):
        fc, fs, cc, cs = carry
        cos_rows, sin_rows = [fc], [fs]
        for jump in range(4):
            jc = jnp.broadcast_to(turn[2 * jump, pl.ds(spin_bin, 1), :], (8, chunk))
            js = jnp.broadcast_to(turn[2 * jump + 1, pl.ds(spin_bin, 1), :], (8, chunk))
            a, b, c, d = jc * fc, js * fs, js * fc, jc * fs
            cos_rows.append(a + b)
            sin_rows.append(c - d)
            if jump < 3:
                cos_rows.append(a - b)
                sin_rows.append(c + d)
        fine = jnp.concatenate([x.astype(jnp.bfloat16) for x in _pairs(cos_rows + sin_rows)], 0)
        spectra = [
            jnp.broadcast_to(spec[row, pl.ds(spin_bin, 1), :], (8, chunk))
            for row in range(2 * beams)
        ]
        coarse_rows = [x * cc for x in spectra] + [x * cs for x in spectra]
        coarse = jnp.concatenate([x.astype(jnp.bfloat16) for x in _pairs(coarse_rows)], 0)
        acc[spin_bin] += lax.dot_general(
            coarse, fine, (((1,), (1,)), ((), ())), preferred_element_type=jnp.float32
        )
        return (
            fc * fine_rc - fs * fine_rs,
            fs * fine_rc + fc * fine_rs,
            cc * coarse_rc - cs * coarse_rs,
            cs * coarse_rc + cc * coarse_rs,
        )

    def some_bins(group, carry):
        for offset in range(UNROLL):
            carry = one_bin(group * UNROLL + offset, carry)
        return carry

    one = jnp.ones((8, chunk), jnp.float32)
    zero = jnp.zeros((8, chunk), jnp.float32)
    lax.fori_loop(0, bins // UNROLL, some_bins, (one, zero, one, zero))

    @pl.when(step == steps - 1)
    def _():
        trials = trials_ref[...]
        count = trials.shape[1]
        cell = lax.shift_right_logical(trials, jnp.int32(7))
        fine_odd = 2 * (trials & (2 * FINE - 1)) - (2 * FINE - 1)
        fine_sign = jnp.where(fine_odd > 0, 1.0, -1.0)
        coarse_sign = jnp.where(cell >= COARSE, 1.0, -1.0)
        coarse_index = jnp.where(cell >= COARSE, cell - COARSE, COARSE - 1 - cell)
        row = lax.broadcasted_iota(jnp.int32, (4 * FINE, count), 0) & (2 * FINE - 1)
        block = lax.shift_right_logical(row & (FINE - 1), jnp.int32(3))
        odd_row = 2 * (row & 7) + 1
        jump = lax.shift_right_logical(block + 1, jnp.int32(1)) * 32
        row_odd = jnp.where((block & 1) == 1, jump - odd_row, jump + odd_row)
        hit = row_odd == jnp.abs(fine_odd)
        pick_cos = jnp.where(hit & (row < FINE), 1.0, 0.0)
        pick_sin = jnp.where(hit & (row >= FINE), fine_sign, 0.0)
        pick = jnp.concatenate([pick_cos, pick_sin], 1).astype(jnp.bfloat16)
        scale = 1.0 / math.sqrt(chan_total)
        coarse_hit = lax.broadcasted_iota(jnp.int32, (COARSE, count), 0) == coarse_index
        mask = jnp.where(coarse_hit, scale, 0.0)
        signed = jnp.where(coarse_hit, scale * coarse_sign, 0.0)

        def pick_bin(spin_bin):
            sums = acc[spin_bin]
            high = sums.astype(jnp.bfloat16)
            low = (sums - high.astype(jnp.float32)).astype(jnp.bfloat16)
            picked = jnp.dot(
                jnp.concatenate([high, low], 1), pick, preferred_element_type=jnp.float32
            )
            parts = picked.reshape(2, 2, beams, COARSE, 2 * count)
            cc, cs = parts[0, ..., :count], parts[0, ..., count:]
            sc, ss = parts[1, ..., :count], parts[1, ..., count:]
            even = cc * mask - ss * signed
            odd_part = sc * signed + cs * mask
            real = jnp.sum(even[0] - odd_part[1], axis=1)
            imag = jnp.sum(odd_part[0] + even[1], axis=1)
            out_ref[spin_bin] = jnp.concatenate([real, imag], 0)

        def pick_some(group, carry):
            for offset in range(3):
                pick_bin(group * 3 + offset)
            return carry

        lax.fori_loop(0, bins // 3, pick_some, 0)


def _pairs(rows):
    return [jnp.concatenate(rows[i : i + 2], 0) for i in range(0, len(rows), 2)]


def share_kernel(n, bins, part_ref, out_ref, power_ref, got, own, gotp, send, recv, psend, precv):
    me = lax.axis_index("chan")
    half = part_ref.shape[1] // 2
    barrier = pltpu.get_barrier_semaphore()

    def greet(hop, carry):
        peer = lax.rem(me + hop, n)
        pl.semaphore_signal(
            barrier, inc=1, device_id={"chan": peer}, device_id_type=pl.DeviceIdType.MESH
        )
        return carry

    lax.fori_loop(1, n, greet, 0)
    pl.semaphore_wait(barrier, n - 1)

    def spread(hop):
        peer = lax.rem(me + hop, n)
        return pltpu.make_async_remote_copy(
            src_ref=part_ref.at[pl.ds(peer * SPIN_DEV, SPIN_DEV)],
            dst_ref=got.at[hop],
            send_sem=send.at[hop],
            recv_sem=recv.at[hop],
            device_id={"chan": peer},
            device_id_type=pl.DeviceIdType.MESH,
        )

    def spread_power(hop):
        peer = lax.rem(me + hop, n)
        return pltpu.make_async_remote_copy(
            src_ref=own,
            dst_ref=gotp.at[hop],
            send_sem=psend.at[hop],
            recv_sem=precv.at[hop],
            device_id={"chan": peer},
            device_id_type=pl.DeviceIdType.MESH,
        )

    def start(hop, carry):
        spread(hop).start()
        return carry

    lax.fori_loop(1, n, start, 0)
    total = part_ref[pl.ds(me * SPIN_DEV, SPIN_DEV)]

    def collect(hop, total):
        spread(hop).wait_recv()
        return total + got[hop]

    total = lax.fori_loop(1, n, collect, total)
    out_ref[...] = total
    squares = jnp.sum(total * total, axis=0)
    own[...] = (squares[:half] + squares[half:]) * (1.0 / bins)

    def start_power(hop, carry):
        spread_power(hop).start()
        return carry

    lax.fori_loop(1, n, start_power, 0)

    def collect_power(hop, total):
        spread_power(hop).wait_recv()
        return total + gotp[hop]

    power_ref[...] = lax.fori_loop(1, n, collect_power, own[...])

    def finish(hop, carry):
        spread(hop).wait_send()
        spread_power(hop).wait_send()
        return carry

    lax.fori_loop(1, n, finish, 0)


def per_device(voltages, delay_step, trials):
    beams, local_chan, samples = voltages.shape
    n = lax.axis_size("chan")
    bins = SPIN_DEV * n
    chan_total = delay_step.shape[0]
    count = trials.shape[0]
    me = lax.axis_index("chan")
    delay = lax.dynamic_slice_in_dim(delay_step, me * local_chan, local_chan).reshape(1, local_chan)
    table = build_table(samples, bins)
    chunk = min(CHUNK, local_chan)
    rows = 2 * beams
    part = pl.pallas_call(
        functools.partial(local_kernel, bins, chan_total),
        out_shape=jax.ShapeDtypeStruct((bins, rows, count), jnp.float32),
        grid=(local_chan // chunk,),
        in_specs=[
            pl.BlockSpec((beams, chunk, samples), lambda i: (0, i, 0)),
            pl.BlockSpec(table.shape, lambda i: (0, 0)),
            pl.BlockSpec((1, chunk), lambda i: (0, i)),
            pl.BlockSpec((1, count), lambda i: (0, 0)),
        ],
        out_specs=pl.BlockSpec((bins, rows, count), lambda i: (0, 0, 0)),
        scratch_shapes=[
            pltpu.VMEM((bins, 2 * rows * COARSE, 2 * FINE), jnp.float32),
            pltpu.VMEM((rows, bins, chunk), jnp.float32),
            pltpu.VMEM((8, bins, chunk), jnp.float32),
        ],
        compiler_params=pltpu.CompilerParams(
            dimension_semantics=("arbitrary",), vmem_limit_bytes=56 * 1024 * 1024
        ),
        cost_estimate=pl.CostEstimate(
            flops=2 * beams * local_chan * samples * table.shape[1],
            bytes_accessed=2 * beams * local_chan * samples,
            transcendentals=0,
        ),
    )(voltages, table, delay, trials.reshape(1, count))
    spectra, power = pl.pallas_call(
        functools.partial(share_kernel, n, bins),
        out_shape=(
            jax.ShapeDtypeStruct((SPIN_DEV, rows, count), jnp.float32),
            jax.ShapeDtypeStruct((beams, count), jnp.float32),
        ),
        in_specs=[pl.BlockSpec(memory_space=pltpu.VMEM)],
        out_specs=(pl.BlockSpec(memory_space=pltpu.VMEM), pl.BlockSpec(memory_space=pltpu.VMEM)),
        scratch_shapes=[
            pltpu.VMEM((n, SPIN_DEV, rows, count), jnp.float32),
            pltpu.VMEM((beams, count), jnp.float32),
            pltpu.VMEM((n, beams, count), jnp.float32),
            pltpu.SemaphoreType.DMA((n,)),
            pltpu.SemaphoreType.DMA((n,)),
            pltpu.SemaphoreType.DMA((n,)),
            pltpu.SemaphoreType.DMA((n,)),
        ],
        compiler_params=pltpu.CompilerParams(collective_id=0, has_side_effects=True),
    )(part)
    own = count // n
    power = lax.dynamic_slice_in_dim(power, me * own, own, axis=1)
    return (spectra.reshape(SPIN_DEV, 2, beams, count), power)


def solution(mesh):
    return jax.shard_map(
        per_device,
        mesh=mesh,
        in_specs=(P("grp", "chan", None), P(), P()),
        out_specs=(P("chan", None, "grp", None), P("grp", "chan")),
        check_vma=False,
    )
```

```python
import functools
import math

import jax
import jax.numpy as jnp
import numpy as np
from jax import lax
from jax.experimental import pallas as pl
from jax.experimental.pallas import tpu as pltpu
from jax.sharding import PartitionSpec as P

SUBSTEPS = 512
SPIN_DEV = 3
CHUNK = 256
FINE = 64
COARSE = 8
UNROLL = 6
MESH = pl.DeviceIdType.MESH


def padded(count):
    return -(-count // 128) * 128


def build_table(samples, bins):
    index = np.arange(samples)[:, None] * np.arange(bins)[None, :] % samples
    angles = index * (2.0 * math.pi / samples)
    table = np.zeros((samples, padded(2 * bins)), np.float32)
    table[:, :bins] = np.cos(angles)
    table[:, bins : 2 * bins] = -np.sin(angles)
    return jnp.asarray(table.astype(jnp.bfloat16))


def unit_phase(product, shift):
    turns = lax.shift_left(product, jnp.int32(shift)).astype(jnp.float32)
    half = turns * (math.pi * 2.0**-32)
    square = half * half
    sine, cosine = jnp.float32(0), jnp.float32(0)
    for power in (11, 9, 7, 5, 3, 1):
        sine = sine * square + (-1.0) ** (power // 2) / math.factorial(power)
    for power in (12, 10, 8, 6, 4, 2, 0):
        cosine = cosine * square + (-1.0) ** (power // 2) / math.factorial(power)
    sine = sine * half
    return 1.0 - 2.0 * sine * sine, 2.0 * sine * cosine


def kernel(
    n, bins, chan_total, v_ref, table_ref, delay_ref, trials_ref, out_ref, power_ref,
    acc, spec, turn, give, got, mine, bound, came, own, gotp,
    give_send, give_recv, send, recv, power_send, power_recv,
):
    beams, chunk, samples = v_ref.shape
    steps = pl.num_programs(0)
    step = pl.program_id(0)
    shift = 32 - (samples * SUBSTEPS * 2).bit_length() + 1
    delay = delay_ref[...]
    me = lax.axis_index("chan")
    barrier = pltpu.get_barrier_semaphore()

    @pl.when(step == 0)
    def _():
        def greet(hop, carry):
            pl.semaphore_signal(
                barrier, inc=1, device_id={"chan": lax.rem(me + hop, n)}, device_id_type=MESH
            )
            return carry

        lax.fori_loop(1, n, greet, 0)
        acc[...] = jnp.zeros_like(acc)

    bin_delay = lax.broadcasted_iota(jnp.int32, (bins, chunk), 0) * delay
    mid_cos, mid_sin = unit_phase(bin_delay * (samples - 1), shift)
    for jump in range(4):
        jump_cos, jump_sin = unit_phase(bin_delay * (32 * (jump + 1)), shift)
        turn[2 * jump] = jump_cos
        turn[2 * jump + 1] = jump_sin
    for beam in range(beams):
        rows = jnp.dot(v_ref[beam], table_ref[...], preferred_element_type=jnp.float32)
        rows = (rows.T * (1.0 / math.sqrt(samples))).astype(jnp.bfloat16).astype(jnp.float32)
        real, imag = rows[:bins], rows[bins : 2 * bins]
        spec[beam] = real * mid_cos - imag * mid_sin
        spec[beams + beam] = real * mid_sin + imag * mid_cos

    odd = 2 * lax.broadcasted_iota(jnp.int32, (8, chunk), 0) + 1
    fine_rc, fine_rs = unit_phase(odd * delay, shift)
    coarse_rc, coarse_rs = unit_phase(odd * (2 * FINE) * delay, shift)

    def one_bin(spin_bin, carry):
        fc, fs, cc, cs = carry
        cos_rows, sin_rows = [fc], [fs]
        for jump in range(4):
            jc = jnp.broadcast_to(turn[2 * jump, pl.ds(spin_bin, 1), :], (8, chunk))
            js = jnp.broadcast_to(turn[2 * jump + 1, pl.ds(spin_bin, 1), :], (8, chunk))
            a, b, c, d = jc * fc, js * fs, js * fc, jc * fs
            cos_rows.append(a + b)
            sin_rows.append(c - d)
            if jump < 3:
                cos_rows.append(a - b)
                sin_rows.append(c + d)
        fine = jnp.concatenate([x.astype(jnp.bfloat16) for x in _pairs(cos_rows + sin_rows)], 0)
        spectra = [
            jnp.broadcast_to(spec[row, pl.ds(spin_bin, 1), :], (8, chunk))
            for row in range(2 * beams)
        ]
        coarse_rows = [x * cc for x in spectra] + [x * cs for x in spectra]
        coarse = jnp.concatenate([x.astype(jnp.bfloat16) for x in _pairs(coarse_rows)], 0)
        acc[spin_bin] += lax.dot_general(
            coarse, fine, (((1,), (1,)), ((), ())), preferred_element_type=jnp.float32
        )
        return (
            fc * fine_rc - fs * fine_rs,
            fs * fine_rc + fc * fine_rs,
            cc * coarse_rc - cs * coarse_rs,
            cs * coarse_rc + cc * coarse_rs,
        )

    def some_bins(group, carry):
        for offset in range(UNROLL):
            carry = one_bin(group * UNROLL + offset, carry)
        return carry

    one = jnp.ones((8, chunk), jnp.float32)
    zero = jnp.zeros((8, chunk), jnp.float32)
    lax.fori_loop(0, bins // UNROLL, some_bins, (one, zero, one, zero))

    @pl.when(step == steps - 1)
    def _():
        trials = trials_ref[...]
        count = trials.shape[1]
        cell = lax.shift_right_logical(trials, jnp.int32(7))
        fine_odd = 2 * (trials & (2 * FINE - 1)) - (2 * FINE - 1)
        fine_sign = jnp.where(fine_odd > 0, 1.0, -1.0)
        coarse_sign = jnp.where(cell >= COARSE, 1.0, -1.0)
        coarse_index = jnp.where(cell >= COARSE, cell - COARSE, COARSE - 1 - cell)
        row = lax.broadcasted_iota(jnp.int32, (4 * FINE, count), 0) & (2 * FINE - 1)
        block = lax.shift_right_logical(row & (FINE - 1), jnp.int32(3))
        odd_row = 2 * (row & 7) + 1
        jump = lax.shift_right_logical(block + 1, jnp.int32(1)) * 32
        row_odd = jnp.where((block & 1) == 1, jump - odd_row, jump + odd_row)
        hit = row_odd == jnp.abs(fine_odd)
        pick_cos = jnp.where(hit & (row < FINE), 1.0, 0.0)
        pick_sin = jnp.where(hit & (row >= FINE), fine_sign, 0.0)
        pick = jnp.concatenate([pick_cos, pick_sin], 1).astype(jnp.bfloat16)
        scale = 1.0 / math.sqrt(chan_total)
        coarse_hit = lax.broadcasted_iota(jnp.int32, (COARSE, count), 0) == coarse_index
        mask = jnp.where(coarse_hit, scale, 0.0)
        signed = jnp.where(coarse_hit, scale * coarse_sign, 0.0)

        def pick_bin(spin_bin):
            sums = acc[spin_bin]
            high = sums.astype(jnp.bfloat16)
            low = (sums - high.astype(jnp.float32)).astype(jnp.bfloat16)
            picked = jnp.dot(
                jnp.concatenate([high, low], 1), pick, preferred_element_type=jnp.float32
            )
            parts = picked.reshape(2, 2, beams, COARSE, 2 * count)
            cc, cs = parts[0, ..., :count], parts[0, ..., count:]
            sc, ss = parts[1, ..., :count], parts[1, ..., count:]
            even = cc * mask - ss * signed
            odd_part = sc * signed + cs * mask
            real = jnp.sum(even[0] - odd_part[1], axis=1)
            imag = jnp.sum(odd_part[0] + even[1], axis=1)
            return jnp.concatenate([real, imag], 0)

        def pick_owner(owner, target):
            for offset in range(SPIN_DEV):
                target[offset] = pick_bin(owner * SPIN_DEV + offset)

        pairs = n // 2
        sibling = me + 1 - 2 * lax.rem(me, 2)

        def to_sibling(hop):
            return pltpu.make_async_remote_copy(
                src_ref=give.at[hop],
                dst_ref=got.at[hop],
                send_sem=give_send.at[hop],
                recv_sem=give_recv.at[hop],
                device_id={"chan": sibling},
                device_id_type=MESH,
            )

        def to_owner(hop):
            return pltpu.make_async_remote_copy(
                src_ref=bound.at[hop],
                dst_ref=came.at[hop],
                send_sem=send.at[hop],
                recv_sem=recv.at[hop],
                device_id={"chan": lax.rem(me + 2 * hop, n)},
                device_id_type=MESH,
            )

        tile_share = 128 // (count // n)

        def to_power(hop):
            peer = lax.rem(me + hop, n)
            return pltpu.make_async_remote_copy(
                src_ref=own.at[peer // tile_share],
                dst_ref=gotp.at[hop],
                send_sem=power_send.at[hop],
                recv_sem=power_recv.at[hop],
                device_id={"chan": peer},
                device_id_type=MESH,
            )

        pl.semaphore_wait(barrier, n - 1)

        def first(hop, carry):
            slot = lax.rem(hop, pairs)
            pick_owner(lax.rem(sibling + 2 * slot, n), give.at[slot])
            to_sibling(slot).start()
            return carry

        def second(hop, carry):
            pick_owner(lax.rem(me + 2 * hop, n), mine)
            to_sibling(hop).wait_recv()
            whole = mine[...] + got[hop]
            half = jnp.concatenate([whole[..., :128], whole[..., 128:]], 1)
            bound[hop] = half.astype(jnp.bfloat16)
            to_owner(hop).start()
            return carry

        lax.fori_loop(1, pairs + 1, first, 0)
        lax.fori_loop(1, pairs, second, 0)
        pick_owner(me, mine)
        to_sibling(0).wait_recv()
        total = mine[...] + got[0]

        def collect(hop, total):
            to_owner(hop).wait_recv()
            half = came[hop].astype(jnp.float32)
            return total + jnp.concatenate([half[:, : 2 * beams], half[:, 2 * beams :]], 2)

        total = lax.fori_loop(1, pairs, collect, total)
        squares = jnp.sum(total * total, axis=0)
        squares = (squares[:beams] + squares[beams:]) * (1.0 / bins)
        for tile in range(count // 128):
            own[tile] = squares[:, tile * 128 : (tile + 1) * 128]

        def start_power(hop, carry):
            to_power(hop).start()
            return carry

        lax.fori_loop(1, n, start_power, 0)
        out_ref[...] = total

        def collect_power(hop, total):
            to_power(hop).wait_recv()
            return total + gotp[hop]

        power_ref[...] = lax.fori_loop(1, n, collect_power, own[me // tile_share])

        def finish_power(hop, carry):
            to_power(hop).wait_send()
            return carry

        def finish(hop, carry):
            to_owner(hop).wait_send()
            to_sibling(hop).wait_send()
            return carry

        lax.fori_loop(1, n, finish_power, 0)
        lax.fori_loop(1, pairs, finish, 0)
        to_sibling(0).wait_send()


def finish_kernel(n, spectra_ref, power_ref, out_ref, own_ref):
    beams, lanes = own_ref.shape
    out_ref[...] = spectra_ref[...].reshape(out_ref.shape)
    place = lax.rem(lax.axis_index("chan"), 128 // lanes)
    power = power_ref[...]
    total = jnp.zeros((beams, lanes), jnp.float32)
    for index in range(128 // lanes):
        total = jnp.where(place == index, power[:, index * lanes : (index + 1) * lanes], total)
    own_ref[...] = total


def _pairs(rows):
    return [jnp.concatenate(rows[i : i + 2], 0) for i in range(0, len(rows), 2)]


def per_device(voltages, delay_step, trials):
    beams, local_chan, samples = voltages.shape
    n = lax.axis_size("chan")
    bins = SPIN_DEV * n
    chan_total = delay_step.shape[0]
    count = trials.shape[0]
    table = build_table(samples, bins)
    chunk = min(CHUNK, local_chan)
    steps = local_chan // chunk
    rows = 2 * beams
    vmem = pltpu.VMEM
    spectra, power = pl.pallas_call(
        functools.partial(kernel, n, bins, chan_total),
        out_shape=(
            jax.ShapeDtypeStruct((SPIN_DEV, rows, count), jnp.float32),
            jax.ShapeDtypeStruct((beams, 128), jnp.float32),
        ),
        grid=(steps,),
        in_specs=[
            pl.BlockSpec((beams, chunk, samples), lambda i: (0, i, 0)),
            pl.BlockSpec(table.shape, lambda i: (0, 0)),
            pl.BlockSpec((1, chunk), lambda i: (0, lax.axis_index("chan") * steps + i)),
            pl.BlockSpec((1, count), lambda i: (0, 0)),
        ],
        out_specs=(
            pl.BlockSpec((SPIN_DEV, rows, count), lambda i: (0, 0, 0)),
            pl.BlockSpec((beams, 128), lambda i: (0, 0)),
        ),
        scratch_shapes=[
            vmem((bins, 2 * rows * COARSE, 2 * FINE), jnp.float32),
            vmem((rows, bins, chunk), jnp.float32),
            vmem((8, bins, chunk), jnp.float32),
            vmem((n // 2, SPIN_DEV, rows, count), jnp.float32),
            vmem((n // 2, SPIN_DEV, rows, count), jnp.float32),
            vmem((SPIN_DEV, rows, count), jnp.float32),
            vmem((n // 2, SPIN_DEV, 2 * rows, count // 2), jnp.bfloat16),
            vmem((n // 2, SPIN_DEV, 2 * rows, count // 2), jnp.bfloat16),
            vmem((count // 128, beams, 128), jnp.float32),
            vmem((n, beams, 128), jnp.float32),
            pltpu.SemaphoreType.DMA((n // 2,)),
            pltpu.SemaphoreType.DMA((n // 2,)),
            pltpu.SemaphoreType.DMA((n // 2,)),
            pltpu.SemaphoreType.DMA((n // 2,)),
            pltpu.SemaphoreType.DMA((n,)),
            pltpu.SemaphoreType.DMA((n,)),
        ],
        compiler_params=pltpu.CompilerParams(
            dimension_semantics=("arbitrary",),
            vmem_limit_bytes=56 * 1024 * 1024,
            collective_id=0,
            has_side_effects=True,
        ),
    )(voltages, table, delay_step.reshape(1, chan_total), trials.reshape(1, count))
    return pl.pallas_call(
        functools.partial(finish_kernel, n),
        out_shape=(
            jax.ShapeDtypeStruct((SPIN_DEV, 2, beams, count), jnp.float32),
            jax.ShapeDtypeStruct((beams, count // n), jnp.float32),
        ),
    )(spectra, power)


def solution(mesh):
    return jax.shard_map(
        per_device,
        mesh=mesh,
        in_specs=(P("grp", "chan", None), P(), P()),
        out_specs=(P("chan", None, "grp", None), P("grp", "chan")),
        check_vma=False,
    )
```

```python
import functools
import math

import jax
import jax.numpy as jnp
import numpy as np
from jax import lax
from jax.experimental import pallas as pl
from jax.experimental.pallas import tpu as pltpu
from jax.sharding import PartitionSpec as P

SUBSTEPS = 512
SPIN_DEV = 3
CHUNK = 256
FINE = 64
COARSE = 8
MESH = pl.DeviceIdType.MESH


def padded(count):
    return -(-count // 128) * 128


def build_table(samples, bins):
    index = np.arange(samples)[:, None] * np.arange(bins)[None, :] % samples
    angles = index * (2.0 * math.pi / samples)
    table = np.zeros((samples, padded(2 * bins)), np.float32)
    table[:, :bins] = np.cos(angles)
    table[:, bins : 2 * bins] = -np.sin(angles)
    return jnp.asarray(table.astype(jnp.bfloat16))


def unit_phase(product, shift):
    turns = lax.shift_left(product, jnp.int32(shift)).astype(jnp.float32)
    half = turns * (math.pi * 2.0**-32)
    square = half * half
    sine, cosine = jnp.float32(0), jnp.float32(0)
    for power in (11, 9, 7, 5, 3, 1):
        sine = sine * square + (-1.0) ** (power // 2) / math.factorial(power)
    for power in (12, 10, 8, 6, 4, 2, 0):
        cosine = cosine * square + (-1.0) ** (power // 2) / math.factorial(power)
    sine = sine * half
    return 1.0 - 2.0 * sine * sine, 2.0 * sine * cosine


def kernel(
    n, bins, chan_total, v_ref, table_ref, delay_ref, full_ref, trials_ref, out_ref, power_ref,
    spec, turn, give, got, mine, bound, came, own, gotp,
    give_send, give_recv, send, recv, power_send, power_recv,
):
    beams, chunk, samples = v_ref.shape
    steps = pl.num_programs(0)
    step = pl.program_id(0)
    shift = 32 - (samples * SUBSTEPS * 2).bit_length() + 1
    me = lax.axis_index("chan")
    barrier = pltpu.get_barrier_semaphore()

    @pl.when(step == 0)
    def _():
        def greet(hop, carry):
            pl.semaphore_signal(
                barrier, inc=1, device_id={"chan": lax.rem(me + hop, n)}, device_id_type=MESH
            )
            return carry

        lax.fori_loop(1, n, greet, 0)

    here = pl.ds(pl.multiple_of(step * chunk, chunk), chunk)
    bin_delay = lax.broadcasted_iota(jnp.int32, (bins, chunk), 0) * delay_ref[...]
    mid_cos, mid_sin = unit_phase(bin_delay * (samples - 1), shift)
    for jump in range(4):
        jump_cos, jump_sin = unit_phase(bin_delay * (32 * (jump + 1)), shift)
        turn[2 * jump, :, here] = jump_cos
        turn[2 * jump + 1, :, here] = jump_sin
    for beam in range(beams):
        rows = jnp.dot(v_ref[beam], table_ref[...], preferred_element_type=jnp.float32)
        rows = (rows.T * (1.0 / math.sqrt(samples))).astype(jnp.bfloat16).astype(jnp.float32)
        real, imag = rows[:bins], rows[bins : 2 * bins]
        spec[beam, :, here] = real * mid_cos - imag * mid_sin
        spec[beams + beam, :, here] = real * mid_sin + imag * mid_cos

    def bin_sums(spin_bin, lanes, fc, fs, cc, cs):
        def spread(ref, row):
            return jnp.broadcast_to(ref[row, pl.ds(spin_bin, 1), lanes], (8, chunk))

        cos_rows, sin_rows = [fc], [fs]
        for jump in range(4):
            jc, js = spread(turn, 2 * jump), spread(turn, 2 * jump + 1)
            a, b, c, d = jc * fc, js * fs, js * fc, jc * fs
            cos_rows.append(a + b)
            sin_rows.append(c - d)
            if jump < 3:
                cos_rows.append(a - b)
                sin_rows.append(c + d)
        fine = jnp.concatenate([x.astype(jnp.bfloat16) for x in _pairs(cos_rows + sin_rows)], 0)
        spectra = [spread(spec, row) for row in range(2 * beams)]
        coarse_rows = [x * cc for x in spectra] + [x * cs for x in spectra]
        coarse = jnp.concatenate([x.astype(jnp.bfloat16) for x in _pairs(coarse_rows)], 0)
        return lax.dot_general(
            coarse, fine, (((1,), (1,)), ((), ())), preferred_element_type=jnp.float32
        )

    def owner_sums(owner):
        odd = 2 * lax.broadcasted_iota(jnp.int32, (8, chunk), 0) + 1
        sums = [0.0] * SPIN_DEV
        for block in range(spec.shape[2] // chunk):
            lanes = slice(block * chunk, (block + 1) * chunk)
            fine_step = odd * full_ref[:, lanes]
            coarse_step = fine_step * (2 * FINE)
            fine_rc, fine_rs = unit_phase(fine_step, shift)
            coarse_rc, coarse_rs = unit_phase(coarse_step, shift)
            fc, fs = unit_phase(fine_step * (owner * SPIN_DEV), shift)
            cc, cs = unit_phase(coarse_step * (owner * SPIN_DEV), shift)
            for offset in range(SPIN_DEV):
                spin_bin = owner * SPIN_DEV + offset
                sums[offset] += bin_sums(spin_bin, lanes, fc, fs, cc, cs)
                if offset < SPIN_DEV - 1:
                    fc, fs = fc * fine_rc - fs * fine_rs, fs * fine_rc + fc * fine_rs
                    cc, cs = cc * coarse_rc - cs * coarse_rs, cs * coarse_rc + cc * coarse_rs
        return sums

    @pl.when(step == steps - 1)
    def _():
        trials = trials_ref[...]
        count = trials.shape[1]
        cell = lax.shift_right_logical(trials, jnp.int32(7))
        fine_odd = 2 * (trials & (2 * FINE - 1)) - (2 * FINE - 1)
        fine_sign = jnp.where(fine_odd > 0, 1.0, -1.0)
        coarse_sign = jnp.where(cell >= COARSE, 1.0, -1.0)
        coarse_index = jnp.where(cell >= COARSE, cell - COARSE, COARSE - 1 - cell)
        row = lax.broadcasted_iota(jnp.int32, (4 * FINE, count), 0) & (2 * FINE - 1)
        block = lax.shift_right_logical(row & (FINE - 1), jnp.int32(3))
        odd_row = 2 * (row & 7) + 1
        jump = lax.shift_right_logical(block + 1, jnp.int32(1)) * 32
        row_odd = jnp.where((block & 1) == 1, jump - odd_row, jump + odd_row)
        hit = row_odd == jnp.abs(fine_odd)
        pick_cos = jnp.where(hit & (row < FINE), 1.0, 0.0)
        pick_sin = jnp.where(hit & (row >= FINE), fine_sign, 0.0)
        pick = jnp.concatenate([pick_cos, pick_sin], 1).astype(jnp.bfloat16)
        scale = 1.0 / math.sqrt(chan_total)
        coarse_hit = lax.broadcasted_iota(jnp.int32, (COARSE, count), 0) == coarse_index
        mask = jnp.where(coarse_hit, scale, 0.0)
        signed = jnp.where(coarse_hit, scale * coarse_sign, 0.0)

        def pick_bin(sums):
            high = sums.astype(jnp.bfloat16)
            low = (sums - high.astype(jnp.float32)).astype(jnp.bfloat16)
            picked = jnp.dot(
                jnp.concatenate([high, low], 1), pick, preferred_element_type=jnp.float32
            )
            parts = picked.reshape(2, 2, beams, COARSE, 2 * count)
            cc, cs = parts[0, ..., :count], parts[0, ..., count:]
            sc, ss = parts[1, ..., :count], parts[1, ..., count:]
            real = (cc[0] - cs[1]) * mask - (ss[0] + sc[1]) * signed
            imag = (cs[0] + cc[1]) * mask + (sc[0] - ss[1]) * signed
            real, imag = jnp.sum(real, axis=1), jnp.sum(imag, axis=1)
            return jnp.concatenate([real, imag], 0)

        def pick_owner(owner, target):
            for offset, sums in enumerate(owner_sums(owner)):
                target[offset] = pick_bin(sums)

        pairs = n // 2
        sibling = me + 1 - 2 * lax.rem(me, 2)

        def to_sibling(hop):
            return pltpu.make_async_remote_copy(
                src_ref=give.at[hop],
                dst_ref=got.at[hop],
                send_sem=give_send.at[hop],
                recv_sem=give_recv.at[hop],
                device_id={"chan": sibling},
                device_id_type=MESH,
            )

        def to_owner(hop):
            return pltpu.make_async_remote_copy(
                src_ref=bound.at[hop],
                dst_ref=came.at[hop],
                send_sem=send.at[hop],
                recv_sem=recv.at[hop],
                device_id={"chan": lax.rem(me + 2 * hop, n)},
                device_id_type=MESH,
            )

        tile_share = 128 // (count // n)

        def to_power(hop):
            peer = lax.rem(me + hop, n)
            return pltpu.make_async_remote_copy(
                src_ref=own.at[peer // tile_share],
                dst_ref=gotp.at[hop],
                send_sem=power_send.at[hop],
                recv_sem=power_recv.at[hop],
                device_id={"chan": peer},
                device_id_type=MESH,
            )

        pl.semaphore_wait(barrier, n - 1)

        def first(hop, carry):
            slot = lax.rem(hop, pairs)
            pick_owner(lax.rem(sibling + 2 * slot, n), give.at[slot])
            to_sibling(slot).start()
            return carry

        def second(hop, carry):
            slot = lax.rem(hop, pairs)
            pick_owner(lax.rem(me + 2 * slot, n), mine)
            to_sibling(slot).wait_recv()

            @pl.when(hop < pairs)
            def _():
                whole = mine[...] + got[hop]
                half = jnp.concatenate([whole[..., :128], whole[..., 128:]], 1)
                bound[hop] = half.astype(jnp.bfloat16)
                to_owner(hop).start()

            return carry

        lax.fori_loop(1, pairs + 1, first, 0)
        lax.fori_loop(1, pairs + 1, second, 0)
        total = mine[...] + got[0]

        def collect(hop, total):
            to_owner(hop).wait_recv()
            half = came[hop].astype(jnp.float32)
            return total + jnp.concatenate([half[:, : 2 * beams], half[:, 2 * beams :]], 2)

        total = lax.fori_loop(1, pairs, collect, total)
        squares = jnp.sum(total * total, axis=0)
        squares = (squares[:beams] + squares[beams:]) * (1.0 / bins)
        for tile in range(count // 128):
            own[tile] = squares[:, tile * 128 : (tile + 1) * 128]

        def start_power(hop, carry):
            to_power(hop).start()
            return carry

        lax.fori_loop(1, n, start_power, 0)
        out_ref[...] = total

        def collect_power(hop, total):
            to_power(hop).wait_recv()
            return total + gotp[hop]

        power_ref[...] = lax.fori_loop(1, n, collect_power, own[me // tile_share])

        def finish_power(hop, carry):
            to_power(hop).wait_send()
            return carry

        def finish(hop, carry):
            to_owner(hop).wait_send()
            to_sibling(hop).wait_send()
            return carry

        lax.fori_loop(1, n, finish_power, 0)
        lax.fori_loop(1, pairs, finish, 0)
        to_sibling(0).wait_send()


def finish_kernel(n, spectra_ref, power_ref, out_ref, own_ref):
    beams, lanes = own_ref.shape
    out_ref[...] = spectra_ref[...].reshape(out_ref.shape)
    place = lax.rem(lax.axis_index("chan"), 128 // lanes)
    power = power_ref[...]
    total = jnp.zeros((beams, lanes), jnp.float32)
    for index in range(128 // lanes):
        total = jnp.where(place == index, power[:, index * lanes : (index + 1) * lanes], total)
    own_ref[...] = total


def _pairs(rows):
    return [jnp.concatenate(rows[i : i + 2], 0) for i in range(0, len(rows), 2)]


def per_device(voltages, delay_step, trials):
    beams, local_chan, samples = voltages.shape
    n = lax.axis_size("chan")
    bins = SPIN_DEV * n
    chan_total = delay_step.shape[0]
    count = trials.shape[0]
    table = build_table(samples, bins)
    chunk = min(CHUNK, local_chan)
    steps = local_chan // chunk
    rows = 2 * beams
    delay = delay_step.reshape(1, chan_total)
    vmem = pltpu.VMEM
    spectra, power = pl.pallas_call(
        functools.partial(kernel, n, bins, chan_total),
        out_shape=(
            jax.ShapeDtypeStruct((SPIN_DEV, rows, count), jnp.float32),
            jax.ShapeDtypeStruct((beams, 128), jnp.float32),
        ),
        grid=(steps,),
        in_specs=[
            pl.BlockSpec((beams, chunk, samples), lambda i: (0, i, 0)),
            pl.BlockSpec(table.shape, lambda i: (0, 0)),
            pl.BlockSpec((1, chunk), lambda i: (0, lax.axis_index("chan") * steps + i)),
            pl.BlockSpec((1, local_chan), lambda i: (0, lax.axis_index("chan"))),
            pl.BlockSpec((1, count), lambda i: (0, 0)),
        ],
        out_specs=(
            pl.BlockSpec((SPIN_DEV, rows, count), lambda i: (0, 0, 0)),
            pl.BlockSpec((beams, 128), lambda i: (0, 0)),
        ),
        scratch_shapes=[
            vmem((rows, bins, local_chan), jnp.float32),
            vmem((8, bins, local_chan), jnp.float32),
            vmem((n // 2, SPIN_DEV, rows, count), jnp.float32),
            vmem((n // 2, SPIN_DEV, rows, count), jnp.float32),
            vmem((SPIN_DEV, rows, count), jnp.float32),
            vmem((n // 2, SPIN_DEV, 2 * rows, count // 2), jnp.bfloat16),
            vmem((n // 2, SPIN_DEV, 2 * rows, count // 2), jnp.bfloat16),
            vmem((count // 128, beams, 128), jnp.float32),
            vmem((n, beams, 128), jnp.float32),
            pltpu.SemaphoreType.DMA((n // 2,)),
            pltpu.SemaphoreType.DMA((n // 2,)),
            pltpu.SemaphoreType.DMA((n // 2,)),
            pltpu.SemaphoreType.DMA((n // 2,)),
            pltpu.SemaphoreType.DMA((n,)),
            pltpu.SemaphoreType.DMA((n,)),
        ],
        compiler_params=pltpu.CompilerParams(
            dimension_semantics=("arbitrary",),
            vmem_limit_bytes=56 * 1024 * 1024,
            collective_id=0,
            has_side_effects=True,
        ),
    )(voltages, table, delay, delay, trials.reshape(1, count))
    return pl.pallas_call(
        functools.partial(finish_kernel, n),
        out_shape=(
            jax.ShapeDtypeStruct((SPIN_DEV, 2, beams, count), jnp.float32),
            jax.ShapeDtypeStruct((beams, count // n), jnp.float32),
        ),
    )(spectra, power)


def solution(mesh):
    return jax.shard_map(
        per_device,
        mesh=mesh,
        in_specs=(P("grp", "chan", None), P(), P()),
        out_specs=(P("chan", None, "grp", None), P("grp", "chan")),
        check_vma=False,
    )
```

```python
import functools
import math

import jax
import jax.numpy as jnp
import numpy as np
from jax import lax
from jax.experimental import pallas as pl
from jax.experimental.pallas import tpu as pltpu
from jax.sharding import PartitionSpec as P

SUBSTEPS = 512
SPIN_DEV = 3
CHUNK = 256
FINE = 64
COARSE = 8
MESH = pl.DeviceIdType.MESH


def padded(count):
    return -(-count // 128) * 128


def build_table(samples, bins):
    index = np.arange(samples)[:, None] * np.arange(bins)[None, :] % samples
    angles = index * (2.0 * math.pi / samples)
    table = np.zeros((samples, padded(2 * bins)), np.float32)
    table[:, :bins] = np.cos(angles)
    table[:, bins : 2 * bins] = -np.sin(angles)
    return jnp.asarray(table.astype(jnp.bfloat16))


def unit_phase(product, shift):
    turns = lax.shift_left(product, jnp.int32(shift)).astype(jnp.float32)
    half = turns * (math.pi * 2.0**-32)
    square = half * half
    sine, cosine = jnp.float32(0), jnp.float32(0)
    for power in (11, 9, 7, 5, 3, 1):
        sine = sine * square + (-1.0) ** (power // 2) / math.factorial(power)
    for power in (12, 10, 8, 6, 4, 2, 0):
        cosine = cosine * square + (-1.0) ** (power // 2) / math.factorial(power)
    sine = sine * half
    return 1.0 - 2.0 * sine * sine, 2.0 * sine * cosine


def kernel(
    n, bins, chan_total, v_ref, table_ref, delay_ref, trials_ref, out_ref, power_ref,
    spec, fine, coarse, give, got, mine, bound, came, own, gotp,
    give_send, give_recv, send, recv, power_send, power_recv,
):
    beams, chunk, samples = v_ref.shape
    steps = pl.num_programs(0)
    step = pl.program_id(0)
    shift = 32 - (samples * SUBSTEPS * 2).bit_length() + 1
    me = lax.axis_index("chan")
    barrier = pltpu.get_barrier_semaphore()

    @pl.when(step == 0)
    def _():
        def greet(hop, carry):
            pl.semaphore_signal(
                barrier, inc=1, device_id={"chan": lax.rem(me + hop, n)}, device_id_type=MESH
            )
            return carry

        lax.fori_loop(1, n, greet, 0)

    here = pl.ds(pl.multiple_of(step * chunk, chunk), chunk)
    bin_delay = lax.broadcasted_iota(jnp.int32, (bins, chunk), 0) * delay_ref[...]
    mid_cos, mid_sin = unit_phase(bin_delay * (samples - 1), shift)
    for beam in range(beams):
        rows = jnp.dot(v_ref[beam], table_ref[...], preferred_element_type=jnp.float32)
        rows = (rows.T * (1.0 / math.sqrt(samples))).astype(jnp.bfloat16).astype(jnp.float32)
        real, imag = rows[:bins], rows[bins : 2 * bins]
        spec[beam, :, here] = real * mid_cos - imag * mid_sin
        spec[beams + beam, :, here] = real * mid_sin + imag * mid_cos

    column = jnp.broadcast_to(delay_ref[...].astype(jnp.float32), (2 * FINE, chunk)).T
    lane = lax.broadcasted_iota(jnp.int32, (chunk, 2 * FINE), 1)
    odd_lane = 2 * (lane & (FINE - 1)) + 1
    fine_cos, fine_sin = unit_phase(odd_lane * column.astype(jnp.int32), shift)
    fine[0, here] = jnp.where(lane < FINE, fine_cos, -fine_sin)
    fine[1, here] = jnp.where(lane < FINE, 1.0, 0.0)
    fine[2, here] = 2.0 * fine_cos
    odd_row = 2 * lax.broadcasted_iota(jnp.int32, (COARSE, chunk), 0) + 1
    coarse_cos, coarse_sin = unit_phase(odd_row * (2 * FINE) * delay_ref[...], shift)
    coarse[0, :, here] = jnp.ones_like(coarse_cos)
    coarse[1, :, here] = jnp.zeros_like(coarse_cos)
    coarse[2, :, here] = coarse_cos
    coarse[3, :, here] = coarse_sin

    def owner_sums(owner):
        sums = [0.0] * SPIN_DEV
        for block in range(spec.shape[2] // chunk):
            lanes = slice(block * chunk, (block + 1) * chunk)
            before, now, twice = fine[0, lanes], fine[1, lanes], fine[2, lanes]
            cc, cs, turn_c, turn_s = (coarse[index, :, lanes] for index in range(4))
            for offset in range(SPIN_DEV):
                spin_bin = owner * SPIN_DEV + offset
                spectra = [
                    jnp.broadcast_to(spec[row, pl.ds(spin_bin, 1), lanes], (8, chunk))
                    for row in range(2 * beams)
                ]
                rows = [x * cc for x in spectra] + [x * cs for x in spectra]
                rows = jnp.concatenate([x.astype(jnp.bfloat16) for x in _pairs(rows)], 0)
                sums[offset] += jnp.dot(
                    rows, now.astype(jnp.bfloat16), preferred_element_type=jnp.float32
                )
                before, now = now, twice * now - before
                cc, cs = cc * turn_c - cs * turn_s, cs * turn_c + cc * turn_s
            fine[0, lanes], fine[1, lanes] = before, now
            coarse[0, :, lanes], coarse[1, :, lanes] = cc, cs
        return sums

    @pl.when(step == steps - 1)
    def _():
        trials = trials_ref[...]
        count = trials.shape[1]
        cell = lax.shift_right_logical(trials, jnp.int32(7))
        fine_odd = 2 * (trials & (2 * FINE - 1)) - (2 * FINE - 1)
        fine_sign = jnp.where(fine_odd > 0, 1.0, -1.0)
        coarse_sign = jnp.where(cell >= COARSE, 1.0, -1.0)
        coarse_index = jnp.where(cell >= COARSE, cell - COARSE, COARSE - 1 - cell)
        row = lax.broadcasted_iota(jnp.int32, (4 * FINE, count), 0) & (2 * FINE - 1)
        row_odd = 2 * (row & (FINE - 1)) + 1
        hit = row_odd == jnp.abs(fine_odd)
        pick_cos = jnp.where(hit & (row < FINE), 1.0, 0.0)
        pick_sin = jnp.where(hit & (row >= FINE), fine_sign, 0.0)
        pick = jnp.concatenate([pick_cos, pick_sin], 1).astype(jnp.bfloat16)
        scale = 1.0 / math.sqrt(chan_total)
        coarse_hit = lax.broadcasted_iota(jnp.int32, (COARSE, count), 0) == coarse_index
        mask = jnp.where(coarse_hit, scale, 0.0)
        signed = jnp.where(coarse_hit, scale * coarse_sign, 0.0)

        def pick_bin(sums):
            high = sums.astype(jnp.bfloat16)
            low = (sums - high.astype(jnp.float32)).astype(jnp.bfloat16)
            picked = jnp.dot(
                jnp.concatenate([high, low], 1), pick, preferred_element_type=jnp.float32
            )
            parts = picked.reshape(2, 2, beams, COARSE, 2 * count)
            cc, cs = parts[0, ..., :count], parts[0, ..., count:]
            sc, ss = parts[1, ..., :count], parts[1, ..., count:]
            real = (cc[0] - cs[1]) * mask - (ss[0] + sc[1]) * signed
            imag = (cs[0] + cc[1]) * mask + (sc[0] - ss[1]) * signed
            real, imag = jnp.sum(real, axis=1), jnp.sum(imag, axis=1)
            return jnp.concatenate([real, imag], 0)

        pairs = n // 2
        side = lax.rem(me, 2)
        sibling = me + 1 - 2 * side
        my_pair = me // 2

        def to_sibling(hop):
            return pltpu.make_async_remote_copy(
                src_ref=give.at[hop],
                dst_ref=got.at[hop],
                send_sem=give_send.at[hop],
                recv_sem=give_recv.at[hop],
                device_id={"chan": sibling},
                device_id_type=MESH,
            )

        def to_owner(pair, slot):
            return pltpu.make_async_remote_copy(
                src_ref=bound.at[pair],
                dst_ref=came.at[slot],
                send_sem=send.at[pair],
                recv_sem=recv.at[slot],
                device_id={"chan": 2 * pair + side},
                device_id_type=MESH,
            )

        tile_share = 128 // (count // n)

        def to_power(hop):
            peer = lax.rem(me + hop, n)
            return pltpu.make_async_remote_copy(
                src_ref=own.at[peer // tile_share],
                dst_ref=gotp.at[hop],
                send_sem=power_send.at[hop],
                recv_sem=power_recv.at[hop],
                device_id={"chan": peer},
                device_id_type=MESH,
            )

        pl.semaphore_wait(barrier, n - 1)

        def pass_on(pair):
            to_sibling(pair).wait_recv()
            whole = mine[pair] + got[pair]
            mine[pair] = whole

            @pl.when(pair != my_pair)
            def _():
                half = jnp.concatenate([whole[..., :128], whole[..., 128:]], 1)
                bound[pair] = half.astype(jnp.bfloat16)
                to_owner(pair, my_pair).start()

        def one_pair(pair, carry):
            even = [pick_bin(sums) for sums in owner_sums(2 * pair)]
            odd = [pick_bin(sums) for sums in owner_sums(2 * pair + 1)]
            for offset in range(SPIN_DEV):
                give[pair, offset] = jnp.where(side == 0, odd[offset], even[offset])
                mine[pair, offset] = jnp.where(side == 0, even[offset], odd[offset])
            to_sibling(pair).start()

            @pl.when(pair > 0)
            def _():
                pass_on(pair - 1)

            return carry

        lax.fori_loop(0, pairs, one_pair, 0)
        pass_on(pairs - 1)

        def collect(hop, total):
            slot = lax.rem(my_pair + hop, pairs)
            to_owner(slot, slot).wait_recv()
            half = came[slot].astype(jnp.float32)
            return total + jnp.concatenate([half[:, : 2 * beams], half[:, 2 * beams :]], 2)

        total = lax.fori_loop(1, pairs, collect, mine[my_pair])
        squares = jnp.sum(total * total, axis=0)
        squares = (squares[:beams] + squares[beams:]) * (1.0 / bins)
        for tile in range(count // 128):
            own[tile] = squares[:, tile * 128 : (tile + 1) * 128]

        def start_power(hop, carry):
            to_power(hop).start()
            return carry

        lax.fori_loop(1, n, start_power, 0)
        out_ref[...] = total

        def collect_power(hop, total):
            to_power(hop).wait_recv()
            return total + gotp[hop]

        power_ref[...] = lax.fori_loop(1, n, collect_power, own[me // tile_share])

        def finish_power(hop, carry):
            to_power(hop).wait_send()
            return carry

        def finish(hop, carry):
            pair = lax.rem(my_pair + hop, pairs)
            to_owner(pair, my_pair).wait_send()
            to_sibling(pair).wait_send()
            return carry

        lax.fori_loop(1, n, finish_power, 0)
        lax.fori_loop(1, pairs, finish, 0)
        to_sibling(my_pair).wait_send()


def finish_kernel(n, spectra_ref, power_ref, out_ref, own_ref):
    beams, lanes = own_ref.shape
    out_ref[...] = spectra_ref[...].reshape(out_ref.shape)
    place = lax.rem(lax.axis_index("chan"), 128 // lanes)
    power = power_ref[...]
    total = jnp.zeros((beams, lanes), jnp.float32)
    for index in range(128 // lanes):
        total = jnp.where(place == index, power[:, index * lanes : (index + 1) * lanes], total)
    own_ref[...] = total


def _pairs(rows):
    return [jnp.concatenate(rows[i : i + 2], 0) for i in range(0, len(rows), 2)]


def per_device(voltages, delay_step, trials):
    beams, local_chan, samples = voltages.shape
    n = lax.axis_size("chan")
    bins = SPIN_DEV * n
    chan_total = delay_step.shape[0]
    count = trials.shape[0]
    table = build_table(samples, bins)
    chunk = min(CHUNK, local_chan)
    steps = local_chan // chunk
    rows = 2 * beams
    delay = delay_step.reshape(1, chan_total)
    vmem = pltpu.VMEM
    spectra, power = pl.pallas_call(
        functools.partial(kernel, n, bins, chan_total),
        out_shape=(
            jax.ShapeDtypeStruct((SPIN_DEV, rows, count), jnp.float32),
            jax.ShapeDtypeStruct((beams, 128), jnp.float32),
        ),
        grid=(steps,),
        in_specs=[
            pl.BlockSpec((beams, chunk, samples), lambda i: (0, i, 0)),
            pl.BlockSpec(table.shape, lambda i: (0, 0)),
            pl.BlockSpec((1, chunk), lambda i: (0, lax.axis_index("chan") * steps + i)),
            pl.BlockSpec((1, count), lambda i: (0, 0)),
        ],
        out_specs=(
            pl.BlockSpec((SPIN_DEV, rows, count), lambda i: (0, 0, 0)),
            pl.BlockSpec((beams, 128), lambda i: (0, 0)),
        ),
        scratch_shapes=[
            vmem((rows, bins, local_chan), jnp.float32),
            vmem((3, local_chan, 2 * FINE), jnp.float32),
            vmem((4, COARSE, local_chan), jnp.float32),
            vmem((n // 2, SPIN_DEV, rows, count), jnp.float32),
            vmem((n // 2, SPIN_DEV, rows, count), jnp.float32),
            vmem((n // 2, SPIN_DEV, rows, count), jnp.float32),
            vmem((n // 2, SPIN_DEV, 2 * rows, count // 2), jnp.bfloat16),
            vmem((n // 2, SPIN_DEV, 2 * rows, count // 2), jnp.bfloat16),
            vmem((count // 128, beams, 128), jnp.float32),
            vmem((n, beams, 128), jnp.float32),
            pltpu.SemaphoreType.DMA((n // 2,)),
            pltpu.SemaphoreType.DMA((n // 2,)),
            pltpu.SemaphoreType.DMA((n // 2,)),
            pltpu.SemaphoreType.DMA((n // 2,)),
            pltpu.SemaphoreType.DMA((n,)),
            pltpu.SemaphoreType.DMA((n,)),
        ],
        compiler_params=pltpu.CompilerParams(
            dimension_semantics=("arbitrary",),
            vmem_limit_bytes=56 * 1024 * 1024,
            collective_id=0,
            has_side_effects=True,
        ),
    )(voltages, table, delay, trials.reshape(1, count))
    return pl.pallas_call(
        functools.partial(finish_kernel, n),
        out_shape=(
            jax.ShapeDtypeStruct((SPIN_DEV, 2, beams, count), jnp.float32),
            jax.ShapeDtypeStruct((beams, count // n), jnp.float32),
        ),
    )(spectra, power)


def solution(mesh):
    return jax.shard_map(
        per_device,
        mesh=mesh,
        in_specs=(P("grp", "chan", None), P(), P()),
        out_specs=(P("chan", None, "grp", None), P("grp", "chan")),
        check_vma=False,
    )
```

```python
import functools
import math

import jax
import jax.numpy as jnp
import numpy as np
from jax import lax
from jax.experimental import pallas as pl
from jax.experimental.pallas import tpu as pltpu
from jax.sharding import PartitionSpec as P

SUBSTEPS = 512
SPIN_DEV = 3
CHUNK = 256
FINE = 64
COARSE = 8
MESH = pl.DeviceIdType.MESH


def padded(count):
    return -(-count // 128) * 128


def build_table(samples, bins):
    index = np.arange(samples)[:, None] * np.arange(bins)[None, :] % samples
    angles = index * (2.0 * math.pi / samples)
    table = np.zeros((samples, padded(2 * bins)), np.float32)
    table[:, :bins] = np.cos(angles)
    table[:, bins : 2 * bins] = -np.sin(angles)
    return jnp.asarray(table.astype(jnp.bfloat16))


def unit_phase(product, shift):
    turns = lax.shift_left(product, jnp.int32(shift)).astype(jnp.float32)
    half = turns * (math.pi * 2.0**-32)
    square = half * half
    sine, cosine = jnp.float32(0), jnp.float32(0)
    for power in (11, 9, 7, 5, 3, 1):
        sine = sine * square + (-1.0) ** (power // 2) / math.factorial(power)
    for power in (12, 10, 8, 6, 4, 2, 0):
        cosine = cosine * square + (-1.0) ** (power // 2) / math.factorial(power)
    sine = sine * half
    return 1.0 - 2.0 * sine * sine, 2.0 * sine * cosine


def kernel(
    n, bins, chan_total, v_ref, table_ref, delay_ref, trials_ref, out_ref, power_ref,
    spec, fine, coarse, left_a, right_a, left_b, right_b, give, got, mine, bound, came, own, gotp,
    give_send, give_recv, send, recv, power_send, power_recv,
):
    beams, chunk, samples = v_ref.shape
    steps = pl.num_programs(0)
    step = pl.program_id(0)
    shift = 32 - (samples * SUBSTEPS * 2).bit_length() + 1
    me = lax.axis_index("chan")
    barrier = pltpu.get_barrier_semaphore()

    @pl.when(step == 0)
    def _():
        def greet(hop, carry):
            pl.semaphore_signal(
                barrier, inc=1, device_id={"chan": lax.rem(me + hop, n)}, device_id_type=MESH
            )
            return carry

        lax.fori_loop(1, n, greet, 0)

    here = pl.ds(pl.multiple_of(step * chunk, chunk), chunk)
    bin_delay = lax.broadcasted_iota(jnp.int32, (bins, chunk), 0) * delay_ref[...]
    mid_cos, mid_sin = unit_phase(bin_delay * (samples - 1), shift)
    every = v_ref[...].reshape(beams * chunk, samples)
    every = jnp.dot(every, table_ref[...], preferred_element_type=jnp.float32)
    for beam in range(beams):
        rows = every[beam * chunk : (beam + 1) * chunk].T
        rows = (rows * (1.0 / math.sqrt(samples))).astype(jnp.bfloat16).astype(jnp.float32)
        real, imag = rows[:bins], rows[bins : 2 * bins]
        turned = real * mid_cos - imag * mid_sin, real * mid_sin + imag * mid_cos
        for kind, values in enumerate(turned):
            place = pl.ds(kind * beams + beam, bins, stride=2 * beams)
            for tile in range(chunk // 128):
                spec[step * (chunk // 128) + tile, place, :] = values[:, tile * 128 : tile * 128 + 128]

    column = jnp.broadcast_to(delay_ref[...].astype(jnp.float32), (2 * FINE, chunk)).T
    lane = lax.broadcasted_iota(jnp.int32, (chunk, 2 * FINE), 1)
    odd_lane = 2 * (lane & (FINE - 1)) + 1
    fine_cos, fine_sin = unit_phase(odd_lane * column.astype(jnp.int32), shift)
    fine[0, here] = jnp.where(lane < FINE, fine_cos, -fine_sin)
    fine[1, here] = jnp.where(lane < FINE, 1.0, 0.0)
    fine[2, here] = 2.0 * fine_cos
    odd_row = 2 * lax.broadcasted_iota(jnp.int32, (COARSE, chunk), 0) + 1
    coarse_cos, coarse_sin = unit_phase(odd_row * (2 * FINE) * delay_ref[...], shift)
    coarse[0, :, here] = jnp.ones_like(coarse_cos)
    coarse[1, :, here] = jnp.zeros_like(coarse_cos)
    coarse[2, :, here] = coarse_cos
    coarse[3, :, here] = coarse_sin

    def build(owner, left, right):
        for tile in range(spec.shape[0]):
            start = tile * 128
            lanes = slice(start, start + 128)
            cc, cs, turn_c, turn_s = (coarse[index, :, lanes] for index in range(4))
            for offset in range(SPIN_DEV):
                at = pl.multiple_of((owner * SPIN_DEV + offset) * (2 * beams), 2 * beams)
                values = spec[tile, pl.ds(at, 2 * beams)]
                for half, wave in enumerate((cc, cs)):
                    for pair in range(beams):
                        rows = [
                            jnp.broadcast_to(values[row : row + 1], (8, 128)) * wave
                            for row in (2 * pair, 2 * pair + 1)
                        ]
                        place = (half * beams + pair) * 16
                        left[offset, place : place + 16, lanes] = jnp.concatenate(rows, 0).astype(
                            jnp.bfloat16
                        )
                cc, cs = cc * turn_c - cs * turn_s, cs * turn_c + cc * turn_s
            coarse[0, :, lanes], coarse[1, :, lanes] = cc, cs
            for piece in range(start, start + 128, 64):
                rows = slice(piece, piece + 64)
                before, now, twice = fine[0, rows], fine[1, rows], fine[2, rows]
                for offset in range(SPIN_DEV):
                    right[offset, rows] = now.astype(jnp.bfloat16)
                    before, now = now, twice * now - before
                fine[0, rows], fine[1, rows] = before, now

    def multiply(left, right):
        return [
            jnp.dot(left[offset], right[offset], preferred_element_type=jnp.float32)
            for offset in range(SPIN_DEV)
        ]

    @pl.when(step == steps - 1)
    def _():
        trials = trials_ref[...]
        count = trials.shape[1]
        cell = lax.shift_right_logical(trials, jnp.int32(7))
        fine_odd = 2 * (trials & (2 * FINE - 1)) - (2 * FINE - 1)
        fine_sign = jnp.where(fine_odd > 0, 1.0, -1.0)
        coarse_sign = jnp.where(cell >= COARSE, 1.0, -1.0)
        coarse_index = jnp.where(cell >= COARSE, cell - COARSE, COARSE - 1 - cell)
        row = lax.broadcasted_iota(jnp.int32, (4 * FINE, count), 0) & (2 * FINE - 1)
        row_odd = 2 * (row & (FINE - 1)) + 1
        hit = row_odd == jnp.abs(fine_odd)
        pick_cos = jnp.where(hit & (row < FINE), 1.0, 0.0)
        pick_sin = jnp.where(hit & (row >= FINE), fine_sign, 0.0)
        pick = jnp.concatenate([pick_cos, pick_sin], 1).astype(jnp.bfloat16)
        scale = 1.0 / math.sqrt(chan_total)
        coarse_hit = lax.broadcasted_iota(jnp.int32, (COARSE, count), 0) == coarse_index
        mask = jnp.where(coarse_hit, scale, 0.0)
        signed = jnp.where(coarse_hit, scale * coarse_sign, 0.0)

        def pick_owner(left, right):
            sums = jnp.concatenate(multiply(left, right), 0)
            high = sums.astype(jnp.bfloat16)
            low = (sums - high.astype(jnp.float32)).astype(jnp.bfloat16)
            picked = jnp.dot(
                jnp.concatenate([high, low], 1), pick, preferred_element_type=jnp.float32
            )
            parts = picked.reshape(SPIN_DEV, 2, 2, beams, COARSE, 2 * count)
            out = []
            for offset in range(SPIN_DEV):
                cc, cs = parts[offset, 0, ..., :count], parts[offset, 0, ..., count:]
                sc, ss = parts[offset, 1, ..., :count], parts[offset, 1, ..., count:]
                real = (cc[0] - cs[1]) * mask - (ss[0] + sc[1]) * signed
                imag = (cs[0] + cc[1]) * mask + (sc[0] - ss[1]) * signed
                out.append(jnp.concatenate([jnp.sum(real, axis=1), jnp.sum(imag, axis=1)], 0))
            return out

        pairs = n // 2
        side = lax.rem(me, 2)
        sibling = me + 1 - 2 * side
        my_pair = me // 2

        def to_sibling(hop):
            return pltpu.make_async_remote_copy(
                src_ref=give.at[hop],
                dst_ref=got.at[hop],
                send_sem=give_send.at[hop],
                recv_sem=give_recv.at[hop],
                device_id={"chan": sibling},
                device_id_type=MESH,
            )

        def to_owner(pair, slot):
            return pltpu.make_async_remote_copy(
                src_ref=bound.at[pair],
                dst_ref=came.at[slot],
                send_sem=send.at[pair],
                recv_sem=recv.at[slot],
                device_id={"chan": 2 * pair + side},
                device_id_type=MESH,
            )

        tile_share = 128 // (count // n)

        def to_power(hop):
            peer = lax.rem(me + hop, n)
            return pltpu.make_async_remote_copy(
                src_ref=own.at[peer // tile_share],
                dst_ref=gotp.at[hop],
                send_sem=power_send.at[hop],
                recv_sem=power_recv.at[hop],
                device_id={"chan": peer},
                device_id_type=MESH,
            )

        pl.semaphore_wait(barrier, n - 1)

        def pass_on(pair):
            to_sibling(pair).wait_recv()
            whole = mine[pair] + got[pair]
            mine[pair] = whole

            @pl.when(pair != my_pair)
            def _():
                half = jnp.concatenate([whole[..., :128], whole[..., 128:]], 1)
                bound[pair] = half.astype(jnp.bfloat16)
                to_owner(pair, my_pair).start()

        def one_pair(pair, carry):
            build(2 * pair + 1, left_b, right_b)
            even = pick_owner(left_a, right_a)
            build(lax.rem(2 * pair + 2, n), left_a, right_a)
            odd = pick_owner(left_b, right_b)
            for offset in range(SPIN_DEV):
                give[pair, offset] = jnp.where(side == 0, odd[offset], even[offset])
                mine[pair, offset] = jnp.where(side == 0, even[offset], odd[offset])
            to_sibling(pair).start()

            @pl.when(pair > 0)
            def _():
                pass_on(pair - 1)

            return carry

        build(0, left_a, right_a)
        lax.fori_loop(0, pairs, one_pair, 0)
        pass_on(pairs - 1)

        def collect(hop, total):
            slot = lax.rem(my_pair + hop, pairs)
            to_owner(slot, slot).wait_recv()
            half = came[slot].astype(jnp.float32)
            return total + jnp.concatenate([half[:, : 2 * beams], half[:, 2 * beams :]], 2)

        total = lax.fori_loop(1, pairs, collect, mine[my_pair])
        squares = jnp.sum(total * total, axis=0)
        squares = (squares[:beams] + squares[beams:]) * (1.0 / bins)
        for tile in range(count // 128):
            own[tile] = squares[:, tile * 128 : (tile + 1) * 128]

        def start_power(hop, carry):
            to_power(hop).start()
            return carry

        lax.fori_loop(1, n, start_power, 0)
        out_ref[...] = total

        def collect_power(hop, total):
            to_power(hop).wait_recv()
            return total + gotp[hop]

        power_ref[...] = lax.fori_loop(1, n, collect_power, own[me // tile_share])

        def finish_power(hop, carry):
            to_power(hop).wait_send()
            return carry

        def finish(hop, carry):
            pair = lax.rem(my_pair + hop, pairs)
            to_owner(pair, my_pair).wait_send()
            to_sibling(pair).wait_send()
            return carry

        lax.fori_loop(1, n, finish_power, 0)
        lax.fori_loop(1, pairs, finish, 0)
        to_sibling(my_pair).wait_send()


def finish_kernel(n, spectra_ref, power_ref, out_ref, own_ref):
    beams, lanes = own_ref.shape
    out_ref[...] = spectra_ref[...].reshape(out_ref.shape)
    place = lax.rem(lax.axis_index("chan"), 128 // lanes)
    power = power_ref[...]
    total = jnp.zeros((beams, lanes), jnp.float32)
    for index in range(128 // lanes):
        total = jnp.where(place == index, power[:, index * lanes : (index + 1) * lanes], total)
    own_ref[...] = total


def per_device(voltages, delay_step, trials):
    beams, local_chan, samples = voltages.shape
    n = lax.axis_size("chan")
    bins = SPIN_DEV * n
    chan_total = delay_step.shape[0]
    count = trials.shape[0]
    table = build_table(samples, bins)
    chunk = min(CHUNK, local_chan)
    steps = local_chan // chunk
    rows = 2 * beams
    delay = delay_step.reshape(1, chan_total)
    vmem = pltpu.VMEM
    spectra, power = pl.pallas_call(
        functools.partial(kernel, n, bins, chan_total),
        out_shape=(
            jax.ShapeDtypeStruct((SPIN_DEV, rows, count), jnp.float32),
            jax.ShapeDtypeStruct((beams, 128), jnp.float32),
        ),
        grid=(steps,),
        in_specs=[
            pl.BlockSpec((beams, chunk, samples), lambda i: (0, i, 0)),
            pl.BlockSpec(table.shape, lambda i: (0, 0)),
            pl.BlockSpec((1, chunk), lambda i: (0, lax.axis_index("chan") * steps + i)),
            pl.BlockSpec((1, count), lambda i: (0, 0)),
        ],
        out_specs=(
            pl.BlockSpec((SPIN_DEV, rows, count), lambda i: (0, 0, 0)),
            pl.BlockSpec((beams, 128), lambda i: (0, 0)),
        ),
        scratch_shapes=[
            vmem((local_chan // 128, bins * rows, 128), jnp.float32),
            vmem((3, local_chan, 2 * FINE), jnp.float32),
            vmem((4, COARSE, local_chan), jnp.float32),
            vmem((SPIN_DEV, 2 * rows * COARSE, local_chan), jnp.bfloat16),
            vmem((SPIN_DEV, local_chan, 2 * FINE), jnp.bfloat16),
            vmem((SPIN_DEV, 2 * rows * COARSE, local_chan), jnp.bfloat16),
            vmem((SPIN_DEV, local_chan, 2 * FINE), jnp.bfloat16),
            vmem((n // 2, SPIN_DEV, rows, count), jnp.float32),
            vmem((n // 2, SPIN_DEV, rows, count), jnp.float32),
            vmem((n // 2, SPIN_DEV, rows, count), jnp.float32),
            vmem((n // 2, SPIN_DEV, 2 * rows, count // 2), jnp.bfloat16),
            vmem((n // 2, SPIN_DEV, 2 * rows, count // 2), jnp.bfloat16),
            vmem((count // 128, beams, 128), jnp.float32),
            vmem((n, beams, 128), jnp.float32),
            pltpu.SemaphoreType.DMA((n // 2,)),
            pltpu.SemaphoreType.DMA((n // 2,)),
            pltpu.SemaphoreType.DMA((n // 2,)),
            pltpu.SemaphoreType.DMA((n // 2,)),
            pltpu.SemaphoreType.DMA((n,)),
            pltpu.SemaphoreType.DMA((n,)),
        ],
        compiler_params=pltpu.CompilerParams(
            dimension_semantics=("arbitrary",),
            vmem_limit_bytes=56 * 1024 * 1024,
            collective_id=0,
            has_side_effects=True,
        ),
    )(voltages, table, delay, trials.reshape(1, count))
    return pl.pallas_call(
        functools.partial(finish_kernel, n),
        out_shape=(
            jax.ShapeDtypeStruct((SPIN_DEV, 2, beams, count), jnp.float32),
            jax.ShapeDtypeStruct((beams, count // n), jnp.float32),
        ),
    )(spectra, power)


def solution(mesh):
    return jax.shard_map(
        per_device,
        mesh=mesh,
        in_specs=(P("grp", "chan", None), P(), P()),
        out_specs=(P("chan", None, "grp", None), P("grp", "chan")),
        check_vma=False,
    )
```

```python
import functools
import math

import jax
import jax.numpy as jnp
import numpy as np
from jax import lax
from jax.experimental import pallas as pl
from jax.experimental.pallas import tpu as pltpu
from jax.sharding import PartitionSpec as P

SUBSTEPS = 512
SPIN_DEV = 3
CHUNK = 256
FINE = 64
COARSE = 8
MESH = pl.DeviceIdType.MESH


def padded(count):
    return -(-count // 128) * 128


def build_table(samples, bins):
    index = np.arange(samples)[:, None] * np.arange(bins)[None, :] % samples
    angles = index * (2.0 * math.pi / samples)
    table = np.zeros((samples, padded(2 * bins)), np.float32)
    table[:, :bins] = np.cos(angles)
    table[:, bins : 2 * bins] = -np.sin(angles)
    return jnp.asarray(table.astype(jnp.bfloat16))


def unit_phase(product, shift):
    turns = lax.shift_left(product, jnp.int32(shift)).astype(jnp.float32)
    half = turns * (math.pi * 2.0**-32)
    square = half * half
    sine, cosine = jnp.float32(0), jnp.float32(0)
    for power in (11, 9, 7, 5, 3, 1):
        sine = sine * square + (-1.0) ** (power // 2) / math.factorial(power)
    for power in (12, 10, 8, 6, 4, 2, 0):
        cosine = cosine * square + (-1.0) ** (power // 2) / math.factorial(power)
    sine = sine * half
    return 1.0 - 2.0 * sine * sine, 2.0 * sine * cosine


def kernel(
    n, bins, chan_total, v_ref, table_ref, delay_ref, trials_ref, out_ref, power_ref,
    spec, fine, coarse, give, got, mine, bound, came, own, gotp,
    give_send, give_recv, send, recv, power_send, power_recv,
):
    beams, chunk, samples = v_ref.shape
    steps = pl.num_programs(0)
    step = pl.program_id(0)
    shift = 32 - (samples * SUBSTEPS * 2).bit_length() + 1
    me = lax.axis_index("chan")
    barrier = pltpu.get_barrier_semaphore()

    @pl.when(step == 0)
    def _():
        def greet(hop, carry):
            pl.semaphore_signal(
                barrier, inc=1, device_id={"chan": lax.rem(me + hop, n)}, device_id_type=MESH
            )
            return carry

        lax.fori_loop(1, n, greet, 0)

    here = pl.ds(pl.multiple_of(step * chunk, chunk), chunk)
    bin_delay = lax.broadcasted_iota(jnp.int32, (bins, chunk), 0) * delay_ref[...]
    mid_cos, mid_sin = unit_phase(bin_delay * (samples - 1), shift)
    for beam in range(beams):
        rows = jnp.dot(v_ref[beam], table_ref[...], preferred_element_type=jnp.float32)
        rows = (rows.T * (1.0 / math.sqrt(samples))).astype(jnp.bfloat16).astype(jnp.float32)
        real, imag = rows[:bins], rows[bins : 2 * bins]
        turned = real * mid_cos - imag * mid_sin, real * mid_sin + imag * mid_cos
        for kind, values in enumerate(turned):
            place = pl.ds(kind * beams + beam, bins, stride=2 * beams)
            for tile in range(chunk // 128):
                spec[step * (chunk // 128) + tile, place, :] = values[:, tile * 128 : tile * 128 + 128]

    column = jnp.broadcast_to(delay_ref[...].astype(jnp.float32), (2 * FINE, chunk)).T
    lane = lax.broadcasted_iota(jnp.int32, (chunk, 2 * FINE), 1)
    odd_lane = 2 * (lane & (FINE - 1)) + 1
    fine_cos, fine_sin = unit_phase(odd_lane * column.astype(jnp.int32), shift)
    fine[0, here] = jnp.where(lane < FINE, fine_cos, -fine_sin)
    fine[1, here] = jnp.where(lane < FINE, 1.0, 0.0)
    fine[2, here] = 2.0 * fine_cos
    odd_row = 2 * lax.broadcasted_iota(jnp.int32, (COARSE, chunk), 0) + 1
    coarse_cos, coarse_sin = unit_phase(odd_row * (2 * FINE) * delay_ref[...], shift)
    coarse[0, :, here] = jnp.ones_like(coarse_cos)
    coarse[1, :, here] = jnp.zeros_like(coarse_cos)
    coarse[2, :, here] = coarse_cos
    coarse[3, :, here] = coarse_sin

    def owner_sums(owner):
        sums = [0.0] * SPIN_DEV
        for block in range(spec.shape[0] * 128 // chunk):
            lanes = slice(block * chunk, (block + 1) * chunk)
            before, now, twice = fine[0, lanes], fine[1, lanes], fine[2, lanes]
            cc, cs, turn_c, turn_s = (coarse[index, :, lanes] for index in range(4))
            for offset in range(SPIN_DEV):
                spin_bin = owner * SPIN_DEV + offset
                at = pl.multiple_of(spin_bin * (2 * beams), 2 * beams)
                tiles = range(block * chunk // 128, (block + 1) * chunk // 128)
                values = jnp.concatenate([spec[tile, pl.ds(at, 2 * beams)] for tile in tiles], 1)
                spectra = [
                    jnp.broadcast_to(values[row : row + 1], (8, chunk)) for row in range(2 * beams)
                ]
                rows = [x * cc for x in spectra] + [x * cs for x in spectra]
                rows = jnp.concatenate([x.astype(jnp.bfloat16) for x in _pairs(rows)], 0)
                sums[offset] += jnp.dot(
                    rows, now.astype(jnp.bfloat16), preferred_element_type=jnp.float32
                )
                before, now = now, twice * now - before
                cc, cs = cc * turn_c - cs * turn_s, cs * turn_c + cc * turn_s
            fine[0, lanes], fine[1, lanes] = before, now
            coarse[0, :, lanes], coarse[1, :, lanes] = cc, cs
        return sums

    @pl.when(step == steps - 1)
    def _():
        trials = trials_ref[...]
        count = trials.shape[1]
        cell = lax.shift_right_logical(trials, jnp.int32(7))
        fine_odd = 2 * (trials & (2 * FINE - 1)) - (2 * FINE - 1)
        fine_sign = jnp.where(fine_odd > 0, 1.0, -1.0)
        coarse_sign = jnp.where(cell >= COARSE, 1.0, -1.0)
        coarse_index = jnp.where(cell >= COARSE, cell - COARSE, COARSE - 1 - cell)
        row = lax.broadcasted_iota(jnp.int32, (4 * FINE, count), 0) & (2 * FINE - 1)
        row_odd = 2 * (row & (FINE - 1)) + 1
        hit = row_odd == jnp.abs(fine_odd)
        pick_cos = jnp.where(hit & (row < FINE), 1.0, 0.0)
        pick_sin = jnp.where(hit & (row >= FINE), fine_sign, 0.0)
        pick = jnp.concatenate([pick_cos, pick_sin], 1).astype(jnp.bfloat16)
        scale = 1.0 / math.sqrt(chan_total)
        coarse_hit = lax.broadcasted_iota(jnp.int32, (COARSE, count), 0) == coarse_index
        mask = jnp.where(coarse_hit, scale, 0.0)
        signed = jnp.where(coarse_hit, scale * coarse_sign, 0.0)

        def pick_bin(sums):
            high = sums.astype(jnp.bfloat16)
            low = (sums - high.astype(jnp.float32)).astype(jnp.bfloat16)
            picked = jnp.dot(
                jnp.concatenate([high, low], 1), pick, preferred_element_type=jnp.float32
            )
            parts = picked.reshape(2, 2, beams, COARSE, 2 * count)
            cc, cs = parts[0, ..., :count], parts[0, ..., count:]
            sc, ss = parts[1, ..., :count], parts[1, ..., count:]
            real = (cc[0] - cs[1]) * mask - (ss[0] + sc[1]) * signed
            imag = (cs[0] + cc[1]) * mask + (sc[0] - ss[1]) * signed
            real, imag = jnp.sum(real, axis=1), jnp.sum(imag, axis=1)
            return jnp.concatenate([real, imag], 0)

        pairs = n // 2
        side = lax.rem(me, 2)
        sibling = me + 1 - 2 * side
        my_pair = me // 2

        def to_sibling(hop):
            return pltpu.make_async_remote_copy(
                src_ref=give.at[hop],
                dst_ref=got.at[hop],
                send_sem=give_send.at[hop],
                recv_sem=give_recv.at[hop],
                device_id={"chan": sibling},
                device_id_type=MESH,
            )

        def to_owner(pair, slot):
            return pltpu.make_async_remote_copy(
                src_ref=bound.at[pair],
                dst_ref=came.at[slot],
                send_sem=send.at[pair],
                recv_sem=recv.at[slot],
                device_id={"chan": 2 * pair + side},
                device_id_type=MESH,
            )

        tile_share = 128 // (count // n)

        def to_power(hop):
            peer = lax.rem(me + hop, n)
            return pltpu.make_async_remote_copy(
                src_ref=own.at[peer // tile_share],
                dst_ref=gotp.at[hop],
                send_sem=power_send.at[hop],
                recv_sem=power_recv.at[hop],
                device_id={"chan": peer},
                device_id_type=MESH,
            )

        pl.semaphore_wait(barrier, n - 1)

        def pass_on(pair):
            to_sibling(pair).wait_recv()
            whole = mine[pair] + got[pair]
            mine[pair] = whole

            @pl.when(pair != my_pair)
            def _():
                half = jnp.concatenate([whole[..., :128], whole[..., 128:]], 1)
                bound[pair] = half.astype(jnp.bfloat16)
                to_owner(pair, my_pair).start()

        def one_pair(pair, carry):
            even = [pick_bin(sums) for sums in owner_sums(2 * pair)]
            odd = [pick_bin(sums) for sums in owner_sums(2 * pair + 1)]
            for offset in range(SPIN_DEV):
                give[pair, offset] = jnp.where(side == 0, odd[offset], even[offset])
                mine[pair, offset] = jnp.where(side == 0, even[offset], odd[offset])
            to_sibling(pair).start()

            @pl.when(pair > 0)
            def _():
                pass_on(pair - 1)

            return carry

        lax.fori_loop(0, pairs, one_pair, 0)
        pass_on(pairs - 1)

        def collect(hop, total):
            slot = lax.rem(my_pair + hop, pairs)
            to_owner(slot, slot).wait_recv()
            half = came[slot].astype(jnp.float32)
            return total + jnp.concatenate([half[:, : 2 * beams], half[:, 2 * beams :]], 2)

        total = lax.fori_loop(1, pairs, collect, mine[my_pair])
        squares = jnp.sum(total * total, axis=0)
        squares = (squares[:beams] + squares[beams:]) * (1.0 / bins)
        for tile in range(count // 128):
            own[tile] = squares[:, tile * 128 : (tile + 1) * 128]

        def start_power(hop, carry):
            to_power(hop).start()
            return carry

        lax.fori_loop(1, n, start_power, 0)
        out_ref[...] = total

        def collect_power(hop, total):
            to_power(hop).wait_recv()
            return total + gotp[hop]

        power_ref[...] = lax.fori_loop(1, n, collect_power, own[me // tile_share])

        def finish_power(hop, carry):
            to_power(hop).wait_send()
            return carry

        def finish(hop, carry):
            pair = lax.rem(my_pair + hop, pairs)
            to_owner(pair, my_pair).wait_send()
            to_sibling(pair).wait_send()
            return carry

        lax.fori_loop(1, n, finish_power, 0)
        lax.fori_loop(1, pairs, finish, 0)
        to_sibling(my_pair).wait_send()


def finish_kernel(n, spectra_ref, power_ref, out_ref, own_ref):
    beams, lanes = own_ref.shape
    out_ref[...] = spectra_ref[...].reshape(out_ref.shape)
    place = lax.rem(lax.axis_index("chan"), 128 // lanes)
    power = power_ref[...]
    total = jnp.zeros((beams, lanes), jnp.float32)
    for index in range(128 // lanes):
        total = jnp.where(place == index, power[:, index * lanes : (index + 1) * lanes], total)
    own_ref[...] = total


def _pairs(rows):
    return [jnp.concatenate(rows[i : i + 2], 0) for i in range(0, len(rows), 2)]


def per_device(voltages, delay_step, trials):
    beams, local_chan, samples = voltages.shape
    n = lax.axis_size("chan")
    bins = SPIN_DEV * n
    chan_total = delay_step.shape[0]
    count = trials.shape[0]
    table = build_table(samples, bins)
    chunk = min(CHUNK, local_chan)
    steps = local_chan // chunk
    rows = 2 * beams
    delay = delay_step.reshape(1, chan_total)
    vmem = pltpu.VMEM
    spectra, power = pl.pallas_call(
        functools.partial(kernel, n, bins, chan_total),
        out_shape=(
            jax.ShapeDtypeStruct((SPIN_DEV, rows, count), jnp.float32),
            jax.ShapeDtypeStruct((beams, 128), jnp.float32),
        ),
        grid=(steps,),
        in_specs=[
            pl.BlockSpec((beams, chunk, samples), lambda i: (0, i, 0)),
            pl.BlockSpec(table.shape, lambda i: (0, 0)),
            pl.BlockSpec((1, chunk), lambda i: (0, lax.axis_index("chan") * steps + i)),
            pl.BlockSpec((1, count), lambda i: (0, 0)),
        ],
        out_specs=(
            pl.BlockSpec((SPIN_DEV, rows, count), lambda i: (0, 0, 0)),
            pl.BlockSpec((beams, 128), lambda i: (0, 0)),
        ),
        scratch_shapes=[
            vmem((local_chan // 128, bins * rows, 128), jnp.float32),
            vmem((3, local_chan, 2 * FINE), jnp.float32),
            vmem((4, COARSE, local_chan), jnp.float32),
            vmem((n // 2, SPIN_DEV, rows, count), jnp.float32),
            vmem((n // 2, SPIN_DEV, rows, count), jnp.float32),
            vmem((n // 2, SPIN_DEV, rows, count), jnp.float32),
            vmem((n // 2, SPIN_DEV, 2 * rows, count // 2), jnp.bfloat16),
            vmem((n // 2, SPIN_DEV, 2 * rows, count // 2), jnp.bfloat16),
            vmem((count // 128, beams, 128), jnp.float32),
            vmem((n, beams, 128), jnp.float32),
            pltpu.SemaphoreType.DMA((n // 2,)),
            pltpu.SemaphoreType.DMA((n // 2,)),
            pltpu.SemaphoreType.DMA((n // 2,)),
            pltpu.SemaphoreType.DMA((n // 2,)),
            pltpu.SemaphoreType.DMA((n,)),
            pltpu.SemaphoreType.DMA((n,)),
        ],
        compiler_params=pltpu.CompilerParams(
            dimension_semantics=("arbitrary",),
            vmem_limit_bytes=56 * 1024 * 1024,
            collective_id=0,
            has_side_effects=True,
        ),
    )(voltages, table, delay, trials.reshape(1, count))
    return pl.pallas_call(
        functools.partial(finish_kernel, n),
        out_shape=(
            jax.ShapeDtypeStruct((SPIN_DEV, 2, beams, count), jnp.float32),
            jax.ShapeDtypeStruct((beams, count // n), jnp.float32),
        ),
    )(spectra, power)


def solution(mesh):
    return jax.shard_map(
        per_device,
        mesh=mesh,
        in_specs=(P("grp", "chan", None), P(), P()),
        out_specs=(P("chan", None, "grp", None), P("grp", "chan")),
        check_vma=False,
    )
```

```python
import functools
import math

import jax
import jax.numpy as jnp
import numpy as np
from jax import lax
from jax.experimental import pallas as pl
from jax.experimental.pallas import tpu as pltpu
from jax.sharding import PartitionSpec as P

SUBSTEPS = 512
SPIN_DEV = 3
CHUNK = 256
FINE = 64
COARSE = 8
MESH = pl.DeviceIdType.MESH


def padded(count):
    return -(-count // 128) * 128


def build_table(samples, bins):
    index = np.arange(samples)[:, None] * np.arange(bins)[None, :] % samples
    angles = index * (2.0 * math.pi / samples)
    table = np.zeros((samples, padded(2 * bins)), np.float32)
    table[:, :bins] = np.cos(angles)
    table[:, bins : 2 * bins] = -np.sin(angles)
    return jnp.asarray(table.astype(jnp.bfloat16))


def unit_phase(product, shift):
    turns = lax.shift_left(product, jnp.int32(shift)).astype(jnp.float32)
    half = turns * (math.pi * 2.0**-32)
    square = half * half
    sine, cosine = jnp.float32(0), jnp.float32(0)
    for power in (11, 9, 7, 5, 3, 1):
        sine = sine * square + (-1.0) ** (power // 2) / math.factorial(power)
    for power in (12, 10, 8, 6, 4, 2, 0):
        cosine = cosine * square + (-1.0) ** (power // 2) / math.factorial(power)
    sine = sine * half
    return 1.0 - 2.0 * sine * sine, 2.0 * sine * cosine


def kernel(
    n, bins, chan_total, v_ref, table_ref, delay_ref, trials_ref, out_ref, power_ref,
    spec, fine, coarse, left_a, right_a, left_b, right_b, give, got, mine, bound, came, own, gotp,
    give_send, give_recv, send, recv, power_send, power_recv,
):
    beams, chunk, samples = v_ref.shape
    steps = pl.num_programs(0)
    step = pl.program_id(0)
    shift = 32 - (samples * SUBSTEPS * 2).bit_length() + 1
    me = lax.axis_index("chan")
    barrier = pltpu.get_barrier_semaphore()

    @pl.when(step == 0)
    def _():
        def greet(hop, carry):
            pl.semaphore_signal(
                barrier, inc=1, device_id={"chan": lax.rem(me + hop, n)}, device_id_type=MESH
            )
            return carry

        lax.fori_loop(1, n, greet, 0)

    here = pl.ds(pl.multiple_of(step * chunk, chunk), chunk)
    bin_delay = lax.broadcasted_iota(jnp.int32, (bins, chunk), 0) * delay_ref[...]
    mid_cos, mid_sin = unit_phase(bin_delay * (samples - 1), shift)
    for beam in range(beams):
        rows = jnp.dot(v_ref[beam], table_ref[...], preferred_element_type=jnp.float32).T
        rows = (rows * (1.0 / math.sqrt(samples))).astype(jnp.bfloat16).astype(jnp.float32)
        real, imag = rows[:bins], rows[bins : 2 * bins]
        turned = real * mid_cos - imag * mid_sin, real * mid_sin + imag * mid_cos
        for kind, values in enumerate(turned):
            place = pl.ds(kind * beams + beam, bins, stride=2 * beams)
            for tile in range(chunk // 128):
                spec[step * (chunk // 128) + tile, place, :] = values[:, tile * 128 : tile * 128 + 128]

    column = jnp.broadcast_to(delay_ref[...].astype(jnp.float32), (2 * FINE, chunk)).T
    lane = lax.broadcasted_iota(jnp.int32, (chunk, 2 * FINE), 1)
    odd_lane = 2 * (lane & (FINE - 1)) + 1
    fine_cos, fine_sin = unit_phase(odd_lane * column.astype(jnp.int32), shift)
    fine[0, here] = jnp.where(lane < FINE, fine_cos, -fine_sin)
    fine[1, here] = jnp.where(lane < FINE, 1.0, 0.0)
    fine[2, here] = 2.0 * fine_cos
    odd_row = 2 * lax.broadcasted_iota(jnp.int32, (COARSE, chunk), 0) + 1
    coarse_cos, coarse_sin = unit_phase(odd_row * (2 * FINE) * delay_ref[...], shift)
    coarse[0, :, here] = jnp.ones_like(coarse_cos)
    coarse[1, :, here] = jnp.zeros_like(coarse_cos)
    coarse[2, :, here] = coarse_cos
    coarse[3, :, here] = coarse_sin

    def build(owner, left, right):
        for tile in range(spec.shape[0]):
            start = tile * 128
            lanes = slice(start, start + 128)
            cc, cs, turn_c, turn_s = (coarse[index, :, lanes] for index in range(4))
            for offset in range(SPIN_DEV):
                at = pl.multiple_of((owner * SPIN_DEV + offset) * (2 * beams), 2 * beams)
                values = spec[tile, pl.ds(at, 2 * beams)]
                for half, wave in enumerate((cc, cs)):
                    for pair in range(beams):
                        rows = [
                            jnp.broadcast_to(values[row : row + 1], (8, 128)) * wave
                            for row in (2 * pair, 2 * pair + 1)
                        ]
                        place = (half * beams + pair) * 16
                        left[offset, place : place + 16, lanes] = jnp.concatenate(rows, 0).astype(
                            jnp.bfloat16
                        )
                cc, cs = cc * turn_c - cs * turn_s, cs * turn_c + cc * turn_s
            coarse[0, :, lanes], coarse[1, :, lanes] = cc, cs
            for piece in range(start, start + 128, 64):
                rows = slice(piece, piece + 64)
                before, now, twice = fine[0, rows], fine[1, rows], fine[2, rows]
                for offset in range(SPIN_DEV):
                    right[offset, rows] = now.astype(jnp.bfloat16)
                    before, now = now, twice * now - before
                fine[0, rows], fine[1, rows] = before, now

    def multiply(left, right):
        return [
            jnp.dot(left[offset], right[offset], preferred_element_type=jnp.float32)
            for offset in range(SPIN_DEV)
        ]

    @pl.when(step == steps - 1)
    def _():
        trials = trials_ref[...]
        count = trials.shape[1]
        cell = lax.shift_right_logical(trials, jnp.int32(7))
        fine_odd = 2 * (trials & (2 * FINE - 1)) - (2 * FINE - 1)
        fine_sign = jnp.where(fine_odd > 0, 1.0, -1.0)
        coarse_sign = jnp.where(cell >= COARSE, 1.0, -1.0)
        coarse_index = jnp.where(cell >= COARSE, cell - COARSE, COARSE - 1 - cell)
        row = lax.broadcasted_iota(jnp.int32, (4 * FINE, count), 0) & (2 * FINE - 1)
        row_odd = 2 * (row & (FINE - 1)) + 1
        hit = row_odd == jnp.abs(fine_odd)
        pick_cos = jnp.where(hit & (row < FINE), 1.0, 0.0)
        pick_sin = jnp.where(hit & (row >= FINE), fine_sign, 0.0)
        pick = jnp.concatenate([pick_cos, pick_sin], 1).astype(jnp.bfloat16)
        scale = 1.0 / math.sqrt(chan_total)
        coarse_hit = lax.broadcasted_iota(jnp.int32, (COARSE, count), 0) == coarse_index
        mask = jnp.where(coarse_hit, scale, 0.0)
        signed = jnp.where(coarse_hit, scale * coarse_sign, 0.0)

        def pick_owner(left, right):
            sums = jnp.concatenate(multiply(left, right), 0)
            high = sums.astype(jnp.bfloat16)
            low = (sums - high.astype(jnp.float32)).astype(jnp.bfloat16)
            picked = jnp.dot(
                jnp.concatenate([high, low], 1), pick, preferred_element_type=jnp.float32
            )
            parts = picked.reshape(SPIN_DEV, 2, 2, beams, COARSE, 2 * count)
            out = []
            for offset in range(SPIN_DEV):
                cc, cs = parts[offset, 0, ..., :count], parts[offset, 0, ..., count:]
                sc, ss = parts[offset, 1, ..., :count], parts[offset, 1, ..., count:]
                real = (cc[0] - cs[1]) * mask - (ss[0] + sc[1]) * signed
                imag = (cs[0] + cc[1]) * mask + (sc[0] - ss[1]) * signed
                out.append(jnp.concatenate([jnp.sum(real, axis=1), jnp.sum(imag, axis=1)], 0))
            return out

        pairs = n // 2
        side = lax.rem(me, 2)
        sibling = me + 1 - 2 * side
        my_pair = me // 2

        def to_sibling(hop):
            return pltpu.make_async_remote_copy(
                src_ref=give.at[hop],
                dst_ref=got.at[hop],
                send_sem=give_send.at[hop],
                recv_sem=give_recv.at[hop],
                device_id={"chan": sibling},
                device_id_type=MESH,
            )

        def to_owner(pair, slot):
            return pltpu.make_async_remote_copy(
                src_ref=bound.at[pair],
                dst_ref=came.at[slot],
                send_sem=send.at[pair],
                recv_sem=recv.at[slot],
                device_id={"chan": 2 * pair + side},
                device_id_type=MESH,
            )

        tile_share = 128 // (count // n)

        def to_power(hop):
            peer = lax.rem(me + hop, n)
            return pltpu.make_async_remote_copy(
                src_ref=own.at[peer // tile_share],
                dst_ref=gotp.at[hop],
                send_sem=power_send.at[hop],
                recv_sem=power_recv.at[hop],
                device_id={"chan": peer},
                device_id_type=MESH,
            )

        pl.semaphore_wait(barrier, n - 1)

        def pass_on(pair):
            to_sibling(pair).wait_recv()
            whole = mine[pair] + got[pair]
            mine[pair] = whole

            @pl.when(pair != my_pair)
            def _():
                half = jnp.concatenate([whole[..., :128], whole[..., 128:]], 1)
                bound[pair] = half.astype(jnp.bfloat16)
                to_owner(pair, my_pair).start()

        def one_pair(pair, carry):
            build(2 * pair + 1, left_b, right_b)
            even = pick_owner(left_a, right_a)
            build(lax.rem(2 * pair + 2, n), left_a, right_a)
            odd = pick_owner(left_b, right_b)
            for offset in range(SPIN_DEV):
                give[pair, offset] = jnp.where(side == 0, odd[offset], even[offset])
                mine[pair, offset] = jnp.where(side == 0, even[offset], odd[offset])
            to_sibling(pair).start()

            @pl.when(pair > 0)
            def _():
                pass_on(pair - 1)

            return carry

        build(0, left_a, right_a)
        lax.fori_loop(0, pairs, one_pair, 0)
        pass_on(pairs - 1)

        def collect(hop, total):
            slot = lax.rem(my_pair + hop, pairs)
            to_owner(slot, slot).wait_recv()
            half = came[slot].astype(jnp.float32)
            return total + jnp.concatenate([half[:, : 2 * beams], half[:, 2 * beams :]], 2)

        total = lax.fori_loop(1, pairs, collect, mine[my_pair])
        squares = jnp.sum(total * total, axis=0)
        squares = (squares[:beams] + squares[beams:]) * (1.0 / bins)
        for tile in range(count // 128):
            own[tile] = squares[:, tile * 128 : (tile + 1) * 128]

        def start_power(hop, carry):
            to_power(hop).start()
            return carry

        lax.fori_loop(1, n, start_power, 0)
        out_ref[...] = total

        def collect_power(hop, total):
            to_power(hop).wait_recv()
            return total + gotp[hop]

        power_ref[...] = lax.fori_loop(1, n, collect_power, own[me // tile_share])

        def finish_power(hop, carry):
            to_power(hop).wait_send()
            return carry

        def finish(hop, carry):
            pair = lax.rem(my_pair + hop, pairs)
            to_owner(pair, my_pair).wait_send()
            to_sibling(pair).wait_send()
            return carry

        lax.fori_loop(1, n, finish_power, 0)
        lax.fori_loop(1, pairs, finish, 0)
        to_sibling(my_pair).wait_send()


def finish_kernel(n, spectra_ref, power_ref, out_ref, own_ref):
    beams, lanes = own_ref.shape
    out_ref[...] = spectra_ref[...].reshape(out_ref.shape)
    place = lax.rem(lax.axis_index("chan"), 128 // lanes)
    power = power_ref[...]
    total = jnp.zeros((beams, lanes), jnp.float32)
    for index in range(128 // lanes):
        total = jnp.where(place == index, power[:, index * lanes : (index + 1) * lanes], total)
    own_ref[...] = total


def per_device(voltages, delay_step, trials):
    beams, local_chan, samples = voltages.shape
    n = lax.axis_size("chan")
    bins = SPIN_DEV * n
    chan_total = delay_step.shape[0]
    count = trials.shape[0]
    table = build_table(samples, bins)
    chunk = min(CHUNK, local_chan)
    steps = local_chan // chunk
    rows = 2 * beams
    delay = delay_step.reshape(1, chan_total)
    vmem = pltpu.VMEM
    spectra, power = pl.pallas_call(
        functools.partial(kernel, n, bins, chan_total),
        out_shape=(
            jax.ShapeDtypeStruct((SPIN_DEV, rows, count), jnp.float32),
            jax.ShapeDtypeStruct((beams, 128), jnp.float32),
        ),
        grid=(steps,),
        in_specs=[
            pl.BlockSpec((beams, chunk, samples), lambda i: (0, i, 0)),
            pl.BlockSpec(table.shape, lambda i: (0, 0)),
            pl.BlockSpec((1, chunk), lambda i: (0, lax.axis_index("chan") * steps + i)),
            pl.BlockSpec((1, count), lambda i: (0, 0)),
        ],
        out_specs=(
            pl.BlockSpec((SPIN_DEV, rows, count), lambda i: (0, 0, 0)),
            pl.BlockSpec((beams, 128), lambda i: (0, 0)),
        ),
        scratch_shapes=[
            vmem((local_chan // 128, bins * rows, 128), jnp.float32),
            vmem((3, local_chan, 2 * FINE), jnp.float32),
            vmem((4, COARSE, local_chan), jnp.float32),
            vmem((SPIN_DEV, 2 * rows * COARSE, local_chan), jnp.bfloat16),
            vmem((SPIN_DEV, local_chan, 2 * FINE), jnp.bfloat16),
            vmem((SPIN_DEV, 2 * rows * COARSE, local_chan), jnp.bfloat16),
            vmem((SPIN_DEV, local_chan, 2 * FINE), jnp.bfloat16),
            vmem((n // 2, SPIN_DEV, rows, count), jnp.float32),
            vmem((n // 2, SPIN_DEV, rows, count), jnp.float32),
            vmem((n // 2, SPIN_DEV, rows, count), jnp.float32),
            vmem((n // 2, SPIN_DEV, 2 * rows, count // 2), jnp.bfloat16),
            vmem((n // 2, SPIN_DEV, 2 * rows, count // 2), jnp.bfloat16),
            vmem((count // 128, beams, 128), jnp.float32),
            vmem((n, beams, 128), jnp.float32),
            pltpu.SemaphoreType.DMA((n // 2,)),
            pltpu.SemaphoreType.DMA((n // 2,)),
            pltpu.SemaphoreType.DMA((n // 2,)),
            pltpu.SemaphoreType.DMA((n // 2,)),
            pltpu.SemaphoreType.DMA((n,)),
            pltpu.SemaphoreType.DMA((n,)),
        ],
        compiler_params=pltpu.CompilerParams(
            dimension_semantics=("arbitrary",),
            vmem_limit_bytes=56 * 1024 * 1024,
            collective_id=0,
            has_side_effects=True,
        ),
    )(voltages, table, delay, trials.reshape(1, count))
    return pl.pallas_call(
        functools.partial(finish_kernel, n),
        out_shape=(
            jax.ShapeDtypeStruct((SPIN_DEV, 2, beams, count), jnp.float32),
            jax.ShapeDtypeStruct((beams, count // n), jnp.float32),
        ),
    )(spectra, power)


def solution(mesh):
    return jax.shard_map(
        per_device,
        mesh=mesh,
        in_specs=(P("grp", "chan", None), P(), P()),
        out_specs=(P("chan", None, "grp", None), P("grp", "chan")),
        check_vma=False,
    )
```

```python
import functools
import math

import jax
import jax.numpy as jnp
import numpy as np
from jax import lax
from jax.experimental import pallas as pl
from jax.experimental.pallas import tpu as pltpu
from jax.sharding import PartitionSpec as P

SUBSTEPS = 512
SPIN_DEV = 3
CHUNK = 256
FINE = 64
COARSE = 8
MESH = pl.DeviceIdType.MESH


def padded(count):
    return -(-count // 128) * 128


def build_table(samples, bins):
    index = np.arange(samples)[:, None] * np.arange(bins)[None, :] % samples
    angles = index * (2.0 * math.pi / samples)
    table = np.zeros((samples, padded(2 * bins)), np.float32)
    table[:, :bins] = np.cos(angles)
    table[:, bins : 2 * bins] = -np.sin(angles)
    return jnp.asarray(table.astype(jnp.bfloat16))


def unit_phase(product, shift):
    turns = lax.shift_left(product, jnp.int32(shift)).astype(jnp.float32)
    half = turns * (math.pi * 2.0**-32)
    square = half * half
    sine, cosine = jnp.float32(0), jnp.float32(0)
    for power in (11, 9, 7, 5, 3, 1):
        sine = sine * square + (-1.0) ** (power // 2) / math.factorial(power)
    for power in (12, 10, 8, 6, 4, 2, 0):
        cosine = cosine * square + (-1.0) ** (power // 2) / math.factorial(power)
    sine = sine * half
    return 1.0 - 2.0 * sine * sine, 2.0 * sine * cosine


def kernel(
    n, bins, chan_total, v_ref, table_ref, delay_ref, trials_ref, out_ref, power_ref,
    spec, fine, coarse, give, got, mine, bound, came, own, gotp,
    give_send, give_recv, send, recv, power_send, power_recv,
):
    beams, chunk, samples = v_ref.shape
    steps = pl.num_programs(0)
    step = pl.program_id(0)
    shift = 32 - (samples * SUBSTEPS * 2).bit_length() + 1
    me = lax.axis_index("chan")
    barrier = pltpu.get_barrier_semaphore()

    @pl.when(step == 0)
    def _():
        def greet(hop, carry):
            pl.semaphore_signal(
                barrier, inc=1, device_id={"chan": lax.rem(me + hop, n)}, device_id_type=MESH
            )
            return carry

        lax.fori_loop(1, n, greet, 0)

    here = pl.ds(pl.multiple_of(step * chunk, chunk), chunk)
    bin_delay = lax.broadcasted_iota(jnp.int32, (bins, chunk), 0) * delay_ref[...]
    mid_cos, mid_sin = unit_phase(bin_delay * (samples - 1), shift)
    for beam in range(beams):
        rows = jnp.dot(v_ref[beam], table_ref[...], preferred_element_type=jnp.float32)
        rows = (rows.T * (1.0 / math.sqrt(samples))).astype(jnp.bfloat16).astype(jnp.float32)
        real, imag = rows[:bins], rows[bins : 2 * bins]
        spec[beam, :, here] = real * mid_cos - imag * mid_sin
        spec[beams + beam, :, here] = real * mid_sin + imag * mid_cos

    column = jnp.broadcast_to(delay_ref[...].astype(jnp.float32), (2 * FINE, chunk)).T
    lane = lax.broadcasted_iota(jnp.int32, (chunk, 2 * FINE), 1)
    odd_lane = 2 * (lane & (FINE - 1)) + 1
    fine_cos, fine_sin = unit_phase(odd_lane * column.astype(jnp.int32), shift)
    fine[0, here] = jnp.where(lane < FINE, fine_cos, -fine_sin)
    fine[1, here] = jnp.where(lane < FINE, 1.0, 0.0)
    fine[2, here] = 2.0 * fine_cos
    odd_row = 2 * lax.broadcasted_iota(jnp.int32, (COARSE, chunk), 0) + 1
    coarse_cos, coarse_sin = unit_phase(odd_row * (2 * FINE) * delay_ref[...], shift)
    coarse[0, :, here] = jnp.ones_like(coarse_cos)
    coarse[1, :, here] = jnp.zeros_like(coarse_cos)
    coarse[2, :, here] = coarse_cos
    coarse[3, :, here] = coarse_sin

    def owner_sums(owner):
        sums = [0.0] * SPIN_DEV
        for block in range(spec.shape[2] // chunk):
            lanes = slice(block * chunk, (block + 1) * chunk)
            before, now, twice = fine[0, lanes], fine[1, lanes], fine[2, lanes]
            cc, cs, turn_c, turn_s = (coarse[index, :, lanes] for index in range(4))
            for offset in range(SPIN_DEV):
                spin_bin = owner * SPIN_DEV + offset
                spectra = [
                    jnp.broadcast_to(spec[row, pl.ds(spin_bin, 1), lanes], (8, chunk))
                    for row in range(2 * beams)
                ]
                rows = [x * cc for x in spectra] + [x * cs for x in spectra]
                rows = jnp.concatenate([x.astype(jnp.bfloat16) for x in _pairs(rows)], 0)
                sums[offset] += jnp.dot(
                    rows, now.astype(jnp.bfloat16), preferred_element_type=jnp.float32
                )
                before, now = now, twice * now - before
                cc, cs = cc * turn_c - cs * turn_s, cs * turn_c + cc * turn_s
            fine[0, lanes], fine[1, lanes] = before, now
            coarse[0, :, lanes], coarse[1, :, lanes] = cc, cs
        return sums

    @pl.when(step == steps - 1)
    def _():
        trials = trials_ref[...]
        count = trials.shape[1]
        cell = lax.shift_right_logical(trials, jnp.int32(7))
        fine_odd = 2 * (trials & (2 * FINE - 1)) - (2 * FINE - 1)
        fine_sign = jnp.where(fine_odd > 0, 1.0, -1.0)
        coarse_sign = jnp.where(cell >= COARSE, 1.0, -1.0)
        coarse_index = jnp.where(cell >= COARSE, cell - COARSE, COARSE - 1 - cell)
        row = lax.broadcasted_iota(jnp.int32, (4 * FINE, count), 0) & (2 * FINE - 1)
        row_odd = 2 * (row & (FINE - 1)) + 1
        hit = row_odd == jnp.abs(fine_odd)
        pick_cos = jnp.where(hit & (row < FINE), 1.0, 0.0)
        pick_sin = jnp.where(hit & (row >= FINE), fine_sign, 0.0)
        pick = jnp.concatenate([pick_cos, pick_sin], 1).astype(jnp.bfloat16)
        scale = 1.0 / math.sqrt(chan_total)
        coarse_hit = lax.broadcasted_iota(jnp.int32, (COARSE, count), 0) == coarse_index
        mask = jnp.where(coarse_hit, scale, 0.0)
        signed = jnp.where(coarse_hit, scale * coarse_sign, 0.0)

        def pick_owner(owner):
            sums = jnp.concatenate(owner_sums(owner), 0)
            high = sums.astype(jnp.bfloat16)
            low = (sums - high.astype(jnp.float32)).astype(jnp.bfloat16)
            picked = jnp.dot(
                jnp.concatenate([high, low], 1), pick, preferred_element_type=jnp.float32
            )
            parts = picked.reshape(SPIN_DEV, 2, 2, beams, COARSE, 2 * count)
            out = []
            for offset in range(SPIN_DEV):
                cc, cs = parts[offset, 0, ..., :count], parts[offset, 0, ..., count:]
                sc, ss = parts[offset, 1, ..., :count], parts[offset, 1, ..., count:]
                real = (cc[0] - cs[1]) * mask - (ss[0] + sc[1]) * signed
                imag = (cs[0] + cc[1]) * mask + (sc[0] - ss[1]) * signed
                out.append(jnp.concatenate([jnp.sum(real, axis=1), jnp.sum(imag, axis=1)], 0))
            return out

        pairs = n // 2
        side = lax.rem(me, 2)
        sibling = me + 1 - 2 * side
        my_pair = me // 2

        def to_sibling(hop):
            return pltpu.make_async_remote_copy(
                src_ref=give.at[hop],
                dst_ref=got.at[hop],
                send_sem=give_send.at[hop],
                recv_sem=give_recv.at[hop],
                device_id={"chan": sibling},
                device_id_type=MESH,
            )

        def to_owner(pair, slot):
            return pltpu.make_async_remote_copy(
                src_ref=bound.at[pair],
                dst_ref=came.at[slot],
                send_sem=send.at[pair],
                recv_sem=recv.at[slot],
                device_id={"chan": 2 * pair + side},
                device_id_type=MESH,
            )

        tile_share = 128 // (count // n)

        def to_power(hop):
            peer = lax.rem(me + hop, n)
            return pltpu.make_async_remote_copy(
                src_ref=own.at[peer // tile_share],
                dst_ref=gotp.at[hop],
                send_sem=power_send.at[hop],
                recv_sem=power_recv.at[hop],
                device_id={"chan": peer},
                device_id_type=MESH,
            )

        pl.semaphore_wait(barrier, n - 1)

        def pass_on(pair):
            to_sibling(pair).wait_recv()
            whole = mine[pair] + got[pair]
            mine[pair] = whole

            @pl.when(pair != my_pair)
            def _():
                half = jnp.concatenate([whole[..., :128], whole[..., 128:]], 1)
                bound[pair] = half.astype(jnp.bfloat16)
                to_owner(pair, my_pair).start()

        def one_pair(pair, carry):
            even = pick_owner(2 * pair)
            odd = pick_owner(2 * pair + 1)
            for offset in range(SPIN_DEV):
                give[pair, offset] = jnp.where(side == 0, odd[offset], even[offset])
                mine[pair, offset] = jnp.where(side == 0, even[offset], odd[offset])
            to_sibling(pair).start()

            @pl.when(pair > 0)
            def _():
                pass_on(pair - 1)

            return carry

        lax.fori_loop(0, pairs, one_pair, 0)
        pass_on(pairs - 1)

        def collect(hop, total):
            slot = lax.rem(my_pair + hop, pairs)
            to_owner(slot, slot).wait_recv()
            half = came[slot].astype(jnp.float32)
            return total + jnp.concatenate([half[:, : 2 * beams], half[:, 2 * beams :]], 2)

        total = lax.fori_loop(1, pairs, collect, mine[my_pair])
        squares = jnp.sum(total * total, axis=0)
        squares = (squares[:beams] + squares[beams:]) * (1.0 / bins)
        for tile in range(count // 128):
            own[tile] = squares[:, tile * 128 : (tile + 1) * 128]

        def start_power(hop, carry):
            to_power(hop).start()
            return carry

        lax.fori_loop(1, n, start_power, 0)
        out_ref[...] = total

        def collect_power(hop, total):
            to_power(hop).wait_recv()
            return total + gotp[hop]

        power_ref[...] = lax.fori_loop(1, n, collect_power, own[me // tile_share])

        def finish_power(hop, carry):
            to_power(hop).wait_send()
            return carry

        def finish(hop, carry):
            pair = lax.rem(my_pair + hop, pairs)
            to_owner(pair, my_pair).wait_send()
            to_sibling(pair).wait_send()
            return carry

        lax.fori_loop(1, n, finish_power, 0)
        lax.fori_loop(1, pairs, finish, 0)
        to_sibling(my_pair).wait_send()


def finish_kernel(n, spectra_ref, power_ref, out_ref, own_ref):
    beams, lanes = own_ref.shape
    out_ref[...] = spectra_ref[...].reshape(out_ref.shape)
    place = lax.rem(lax.axis_index("chan"), 128 // lanes)
    power = power_ref[...]
    total = jnp.zeros((beams, lanes), jnp.float32)
    for index in range(128 // lanes):
        total = jnp.where(place == index, power[:, index * lanes : (index + 1) * lanes], total)
    own_ref[...] = total


def _pairs(rows):
    return [jnp.concatenate(rows[i : i + 2], 0) for i in range(0, len(rows), 2)]


def per_device(voltages, delay_step, trials):
    beams, local_chan, samples = voltages.shape
    n = lax.axis_size("chan")
    bins = SPIN_DEV * n
    chan_total = delay_step.shape[0]
    count = trials.shape[0]
    table = build_table(samples, bins)
    chunk = min(CHUNK, local_chan)
    steps = local_chan // chunk
    rows = 2 * beams
    delay = delay_step.reshape(1, chan_total)
    vmem = pltpu.VMEM
    spectra, power = pl.pallas_call(
        functools.partial(kernel, n, bins, chan_total),
        out_shape=(
            jax.ShapeDtypeStruct((SPIN_DEV, rows, count), jnp.float32),
            jax.ShapeDtypeStruct((beams, 128), jnp.float32),
        ),
        grid=(steps,),
        in_specs=[
            pl.BlockSpec((beams, chunk, samples), lambda i: (0, i, 0)),
            pl.BlockSpec(table.shape, lambda i: (0, 0)),
            pl.BlockSpec((1, chunk), lambda i: (0, lax.axis_index("chan") * steps + i)),
            pl.BlockSpec((1, count), lambda i: (0, 0)),
        ],
        out_specs=(
            pl.BlockSpec((SPIN_DEV, rows, count), lambda i: (0, 0, 0)),
            pl.BlockSpec((beams, 128), lambda i: (0, 0)),
        ),
        scratch_shapes=[
            vmem((rows, bins, local_chan), jnp.float32),
            vmem((3, local_chan, 2 * FINE), jnp.float32),
            vmem((4, COARSE, local_chan), jnp.float32),
            vmem((n // 2, SPIN_DEV, rows, count), jnp.float32),
            vmem((n // 2, SPIN_DEV, rows, count), jnp.float32),
            vmem((n // 2, SPIN_DEV, rows, count), jnp.float32),
            vmem((n // 2, SPIN_DEV, 2 * rows, count // 2), jnp.bfloat16),
            vmem((n // 2, SPIN_DEV, 2 * rows, count // 2), jnp.bfloat16),
            vmem((count // 128, beams, 128), jnp.float32),
            vmem((n, beams, 128), jnp.float32),
            pltpu.SemaphoreType.DMA((n // 2,)),
            pltpu.SemaphoreType.DMA((n // 2,)),
            pltpu.SemaphoreType.DMA((n // 2,)),
            pltpu.SemaphoreType.DMA((n // 2,)),
            pltpu.SemaphoreType.DMA((n,)),
            pltpu.SemaphoreType.DMA((n,)),
        ],
        compiler_params=pltpu.CompilerParams(
            dimension_semantics=("arbitrary",),
            vmem_limit_bytes=56 * 1024 * 1024,
            collective_id=0,
            has_side_effects=True,
        ),
    )(voltages, table, delay, trials.reshape(1, count))
    return pl.pallas_call(
        functools.partial(finish_kernel, n),
        out_shape=(
            jax.ShapeDtypeStruct((SPIN_DEV, 2, beams, count), jnp.float32),
            jax.ShapeDtypeStruct((beams, count // n), jnp.float32),
        ),
    )(spectra, power)


def solution(mesh):
    return jax.shard_map(
        per_device,
        mesh=mesh,
        in_specs=(P("grp", "chan", None), P(), P()),
        out_specs=(P("chan", None, "grp", None), P("grp", "chan")),
        check_vma=False,
    )
```
